128 devices in a mesh: lat: 8 (over z_hi, y), lon: 16 (over z_lo, x, core).
Axes of the slice: x: 4, y: 4, z: 4 (z_hi: 2, z_lo: 2; z = z_hi * 2 + z_lo), core: 2. Of those that a mesh axis runs over, the one named last changes fastest.
Arguments:
- fields: bfloat16 [8, 192, 192, 192], P(None, 'lat', 'lon'), may hold values from -6 to 6
- cotangent: bfloat16 [8, 192, 192, 192], P(None, 'lat', 'lon'), may hold values from -6 to 6
- norm_gain: float32 [192], replicated, may hold values from 0.1 to 1.9
- qkv_weight: bfloat16 [192, 576], replicated, may hold values from -0.4375 to 0.4375
- proj_weight: bfloat16 [192, 192], replicated, may hold values from -0.4375 to 0.4375
- bias_table: bfloat16 [21, 6, 144, 144], P(None, None, 'lon'), may hold values from -4 to 240
- window_types: int32 [16], replicated, may hold values from 0 to 20
- valid_mask: int32 [192, 192], replicated, may hold values from 0 to 1, as said below
Outputs:
- mixed_out: bfloat16 [8, 192, 192, 192], P(None, 'lat', 'lon')
- grad_fields: bfloat16 [8, 192, 192, 192], P(None, 'lat', 'lon')
- grad_bias: float32 [16, 6, 144, 144], P('lat', None, 'lon')
The draws below stay inside these ranges and needn't reach their ends.
Inputs may be any that keep to these rules, and one draw needn't show every extreme that they name: valid_mask is 1 outside the first three and the last three latitude rows.
All inputs are finite; a program needn't handle non-finite values.
Results may differ from the reference program's by a relative error of at most 0.022.
Values may be sent and summed in bfloat16 or wider, within the bound.
No kernel may reach another device: no remote copies, remote signals or barrier semaphores. Data moves between devices by JAX's collectives and lax.ppermute only.
A program may use at most 128 MiB of HBM per device.

```python
import jax
import jax.numpy as jnp
from jax import lax

Z = 8
C = 192
HEADS = 6
TYPES = 21
WZ = 2
WLAT = 12
WLON = 6
WIN = 144
SLAT = 6
SLON = 3
NLAT = 192
NLON = 192
NLATWIN = 16


def draw_valid_mask(key, part):
    key = jax.random.fold_in(key, 7)
    lat_rows = jnp.arange(NLAT)
    coin_flip = jax.random.randint(key, (NLAT, NLON), 0, 2)
    polar_band = (lat_rows < 3) | (lat_rows >= NLAT - 3)
    return jnp.where(polar_band[:, None], coin_flip, 1).astype(jnp.int32)


def draw_bias_table(key, part):
    key = jax.random.fold_in(key, 11)
    key_base = jax.random.fold_in(key, 0)
    table_shape = (TYPES, HEADS, WIN, WIN)
    bias_values = jnp.clip(jax.random.normal(key_base, table_shape, jnp.float32), -4.0, 4.0)
    return bias_values.astype(jnp.bfloat16)


def set_ends(result, key, smallest, largest):
    index_at = [jax.random.randint(jax.random.fold_in(key, axis), (), 0, length) for axis, length in enumerate(result.shape)]
    widest = result.shape.index(max(result.shape))
    beside = index_at[:widest] + [(index_at[widest] + 1) % result.shape[widest]] + index_at[widest + 1:]
    return result.at[tuple(index_at)].set(smallest).at[tuple(beside)].set(largest)


def level_of(stream_key, dims, cuts, smallest, top_value):
    gain, own = 1.0, jax.random.fold_in(stream_key, 6)
    for dim, parts in cuts:
        steps = jnp.exp(jax.random.uniform(jax.random.fold_in(own, dim), (parts,), jnp.float32, smallest / len(cuts), top_value / len(cuts)))
        gain = gain * jnp.repeat(steps, dims[dim] // parts).reshape([-1 if axis == dim else 1 for axis in range(len(dims))])
    return gain


def centred(rng, dims, spread, bound, cuts=(), kind=jnp.bfloat16):
    result = spread * jax.random.normal(rng, dims, jnp.float32)
    if cuts:
        result = result * level_of(rng, dims, cuts, -0.22, 0.18)
    return jnp.clip(result, -bound, bound).astype(kind)


def setup_inputs(seed: int = 0) -> dict:
    seeds = jax.random.split(jax.random.key(seed), 9)
    return {
        "fields": centred(seeds[0], (Z, NLAT, NLON, C), 1.0, 6.0, ((1, 8), (2, 16))),
        "cotangent": centred(seeds[1], (Z, NLAT, NLON, C), 1.0, 6.0, ((1, 8), (2, 16))),
        "norm_gain": jnp.clip(1.0 + 0.18 * jax.random.normal(seeds[2], (C,), jnp.float32), 0.1, 1.9),
        "qkv_weight": centred(seeds[3], (C, 3 * C), C ** -0.5, 0.4375),
        "proj_weight": centred(seeds[4], (C, C), C ** -0.5, 0.4375),
        "bias_table": draw_bias_table(jax.random.fold_in(seeds[8], 71), 0),
        "window_types": set_ends(jax.random.randint(seeds[6], (NLATWIN,), 0, TYPES), jax.random.fold_in(seeds[6], 1), 0, TYPES - 1).astype(jnp.int32),
        "valid_mask": draw_valid_mask(jax.random.fold_in(seeds[8], 71), 0),
    }


NEGATIVE = -1e+30
EPSILON = 1e-05

def product(pattern, operand_a, operand_b):
    return jnp.einsum(pattern, operand_a.astype(jnp.float32), operand_b.astype(jnp.float32))

def to_windows(per_cell):
    levels, lat_cells, lon_cells, channels = per_cell.shape
    blocks = per_cell.reshape(levels // WZ, WZ, lat_cells, lon_cells // WLON, WLON, channels)
    blocks = blocks.transpose(0, 3, 1, 2, 4, 5)
    return blocks.reshape(levels // WZ * (lon_cells // WLON), WZ * lat_cells * WLON, channels)

def from_windows(per_cell, levels, lat_cells, lon_cells):
    channels = per_cell.shape[-1]
    blocks = per_cell.reshape(levels // WZ, lon_cells // WLON, WZ, lat_cells, WLON, channels)
    return blocks.transpose(0, 2, 3, 1, 4, 5).reshape(levels, lat_cells, lon_cells, channels)

def slab_pass(field_slab, cot_slab, norm_gain, qkv_weight, proj_weight, bias_rows, key_ok, region):
    levels, lat_cells, lon_cells, features = field_slab.shape
    head_dim = features // HEADS
    scaling = float(head_dim) ** (-0.5)
    field_wide = field_slab.astype(jnp.float32)
    center_mean = lax.optimization_barrier(jnp.mean(field_wide, axis=-1, keepdims=True))
    centered = field_wide - center_mean
    variance = lax.optimization_barrier(jnp.mean(centered * centered, axis=-1, keepdims=True))
    inverse_std = lax.rsqrt(variance + EPSILON)
    hat_field = centered * inverse_std
    normed = (hat_field * norm_gain).astype(jnp.bfloat16)
    packed = jnp.dot(normed.reshape(-1, features), qkv_weight, preferred_element_type=jnp.float32).astype(jnp.bfloat16)
    windowed = to_windows(packed.reshape(levels, lat_cells, lon_cells, 3 * features))
    windows = windowed.shape[0]
    tokens = windowed.shape[1]
    queries = windowed[..., :features].reshape(windows, tokens, HEADS, head_dim)
    key_heads = windowed[..., features:2 * features].reshape(windows, tokens, HEADS, head_dim)
    values = windowed[..., 2 * features:].reshape(windows, tokens, HEADS, head_dim)
    key_valid = to_windows(key_ok[..., None])[..., 0]
    regions = jnp.broadcast_to(region[None, :, None, None], (levels, lat_cells, lon_cells, 1))
    key_region = to_windows(regions)[..., 0]
    allowed = key_valid[:, None, :] & (key_region[:, :, None] == key_region[:, None, :])
    scores = product('wihd,wjhd->whij', queries, key_heads) * scaling + bias_rows.astype(jnp.float32)[None]
    scores = jnp.where(allowed[:, None], scores, NEGATIVE)
    row_max = lax.optimization_barrier(jnp.max(scores, axis=-1, keepdims=True))
    exponent = jnp.exp(scores - row_max)
    soft_full = exponent / lax.optimization_barrier(jnp.sum(exponent, axis=-1, keepdims=True))
    soft_bf = soft_full.astype(jnp.bfloat16)
    attended = product('whij,wjhd->wihd', soft_bf, values).astype(jnp.bfloat16).reshape(-1, features)
    projected = jnp.dot(attended, proj_weight, preferred_element_type=jnp.float32).astype(jnp.bfloat16)
    proj_slab = from_windows(projected.reshape(windows, tokens, features), levels, lat_cells, lon_cells)
    grad_projected = to_windows(cot_slab).reshape(-1, features)
    grad_attended = jnp.dot(grad_projected, proj_weight.T, preferred_element_type=jnp.float32).astype(jnp.bfloat16)
    grad_attended = grad_attended.reshape(windows, tokens, HEADS, head_dim)
    grad_soft = product('wihd,wjhd->whij', grad_attended, values)
    grad_values = product('whij,wihd->wjhd', soft_bf, grad_attended).astype(jnp.bfloat16)
    grad_scores = soft_full * (grad_soft - lax.optimization_barrier(jnp.sum(soft_full * grad_soft, axis=-1, keepdims=True)))
    bias_part = lax.optimization_barrier(jnp.sum(grad_scores, axis=0))
    grad_scores_bf = grad_scores.astype(jnp.bfloat16)
    grad_queries = (product('whij,wjhd->wihd', grad_scores_bf, key_heads) * scaling).astype(jnp.bfloat16)
    grad_keys = (product('whij,wihd->wjhd', grad_scores_bf, queries) * scaling).astype(jnp.bfloat16)
    grad_packed = jnp.concatenate([grad_queries.reshape(windows, tokens, features), grad_keys.reshape(windows, tokens, features), grad_values.reshape(windows, tokens, features)], axis=-1)
    grad_packed = from_windows(grad_packed, levels, lat_cells, lon_cells).reshape(-1, 3 * features)
    grad_normed = jnp.dot(grad_packed, qkv_weight.T, preferred_element_type=jnp.float32).reshape(levels, lat_cells, lon_cells, features)
    grad_hatted = grad_normed * norm_gain
    grad_field = inverse_std * (grad_hatted - lax.optimization_barrier(jnp.mean(grad_hatted, axis=-1, keepdims=True)) - hat_field * lax.optimization_barrier(jnp.mean(grad_hatted * hat_field, axis=-1, keepdims=True)))
    return (proj_slab, grad_field.astype(jnp.bfloat16), bias_part)

def reference(fields, cotangent, norm_gain, qkv_weight, proj_weight, bias_table, window_types, valid_mask):
    shifted_field = jnp.roll(fields, (-SLAT, -SLON), (1, 2))
    shifted_cot = jnp.roll(cotangent, (-SLAT, -SLON), (1, 2))
    key_field = jnp.roll(valid_mask, (-SLAT, -SLON), (0, 1)) == 1

    def slab_step(window):
        row_start = (window * WLAT).astype(jnp.int32)
        field_slab = lax.dynamic_slice_in_dim(shifted_field, row_start, WLAT, 1)
        cot_slab = lax.dynamic_slice_in_dim(shifted_cot, row_start, WLAT, 1)
        ok_rows = lax.dynamic_slice_in_dim(key_field, row_start, WLAT, 0)
        key_ok = jnp.broadcast_to(ok_rows[None], (Z, WLAT, NLON))
        region = row_start + jnp.arange(WLAT, dtype=jnp.int32) >= NLAT - SLAT
        bias_rows = lax.dynamic_index_in_dim(bias_table, window_types[window].astype(jnp.int32), 0, keepdims=False)
        return slab_pass(field_slab, cot_slab, norm_gain, qkv_weight, proj_weight, bias_rows, key_ok, region)
    proj_slabs, grad_slabs, grad_bias = lax.map(slab_step, jnp.arange(NLATWIN, dtype=jnp.int32))
    proj_shift = proj_slabs.transpose(1, 0, 2, 3, 4).reshape(Z, NLAT, NLON, C)
    grad_shift = grad_slabs.transpose(1, 0, 2, 3, 4).reshape(Z, NLAT, NLON, C)
    proj_own = jnp.roll(proj_shift, (SLAT, SLON), (1, 2))
    grad_own = jnp.roll(grad_shift, (SLAT, SLON), (1, 2))
    mixed_out = (fields.astype(jnp.float32) + proj_own.astype(jnp.float32)).astype(jnp.bfloat16)
    grad_fields = (cotangent.astype(jnp.float32) + grad_own.astype(jnp.float32)).astype(jnp.bfloat16)
    return (mixed_out, grad_fields, grad_bias)
```

```python
import functools

import jax
import jax.numpy as jnp
import numpy as np
from jax import lax
from jax.experimental import pallas as pl
from jax.experimental.pallas import tpu as pltpu
from jax.sharding import PartitionSpec as P

HEADS = 6
WZ = 2
WLAT = 12
WLON = 6
WIN = 144
SLAT = 6
SLON = 3
HEAD_DIM = 32
MAIN = 128
REST = WIN - MAIN
LANES = 896
ROWS = 64

NEGATIVE = -1e30
EPSILON = 1e-05
LOG2E = 1.4426950408889634
SCALE = float(HEAD_DIM) ** (-0.5)

F32 = jnp.float32
BF16 = jnp.bfloat16


def nn(a, b):
    return lax.dot_general(a, b, (((1,), (0,)), ((), ())), preferred_element_type=F32)


def nt(a, b):
    return lax.dot_general(a, b, (((1,), (1,)), ((), ())), preferred_element_type=F32)


def tn(a, b):
    return lax.dot_general(a, b, (((0,), (0,)), ((), ())), preferred_element_type=F32)


def lane_of(head, query):
    return np.where(query < MAIN, head * MAIN + query, HEADS * MAIN + head * REST + query - MAIN)


def window_picks():
    pick = np.zeros((2, WIN, WZ, WLAT, 16), np.float32)
    for w in range(2):
        for t in range(WIN):
            z, r, c = t // (WLAT * WLON), (t // WLON) % WLAT, t % WLON
            pick[w, t, z, r, SLON + WLON * w + c] = 1
    return pick.reshape(2, WIN, WZ * WLAT * 16)


def bias_picks(parts):
    per = WIN // parts
    pick = np.zeros((parts, ROWS, LANES), np.float32)
    for k in range(parts):
        for h in range(HEADS):
            for r in range(per):
                pick[k, h * per + r, lane_of(h, k * per + r)] = 1
    return pick.reshape(parts * ROWS, LANES)


def head_blocks(tokens, head_masks):
    pieces = [tokens[:MAIN] * head_masks[h] for h in range(HEADS)]
    pieces += [tokens[MAIN:] * head_masks[h] for h in range(HEADS)]
    pieces.append(jnp.zeros((LANES - HEADS * WIN, tokens.shape[1]), tokens.dtype))
    return jnp.concatenate(pieces, axis=0)


def own_heads(wide):
    main, rest = [], []
    for h in range(HEADS):
        rows = wide[h * HEAD_DIM : (h + 1) * HEAD_DIM]
        main.append(rows[:, h * MAIN : (h + 1) * MAIN])
        left = HEADS * MAIN + h * REST
        rest.append(rows[:, left : left + REST])
    return jnp.concatenate(
        [jnp.concatenate(main, axis=0), jnp.concatenate(rest, axis=0)], axis=1
    )


def kernel(
    at_ref,
    fields_ref,
    cot_ref,
    east_f_ref,
    east_c_ref,
    south_f_ref,
    south_c_ref,
    corner_f_ref,
    corner_c_ref,
    gain_ref,
    qkv_ref,
    proj_ref,
    bias_ref,
    valid_ref,
    pick_ref,
    unpick_ref,
    bias_pick_ref,
    eye_ref,
    proj_out_ref,
    grad_out_ref,
    bias_out_ref,
    weights,
    bias_t,
    bias_sum,
    tile,
):
    step = pl.program_id(0)
    features = fields_ref.shape[-1]

    @pl.when(step == 0)
    def prepare():
        eye = eye_ref[...]
        for n in range(3):
            weights[n] = qkv_ref[:, n * features : (n + 1) * features]
        weights[3] = nt(eye, weights[1]).astype(BF16)
        weights[4] = nt(eye, weights[2]).astype(BF16)
        weights[5] = nt(eye, proj_ref[...]).astype(BF16)
        bias_sum[...] = jnp.zeros_like(bias_sum)
        tile[...] = jnp.zeros_like(tile)
        for b in range(2):
            table = bias_ref[:, b].reshape(-1, WIN)
            wide = tn(table, bias_pick_ref[...]) * LOG2E
            if b == 0:
                bias_t[0] = wide
            else:
                key = lax.broadcasted_iota(jnp.int32, (WIN, 1), 0)
                lane = lax.broadcasted_iota(jnp.int32, (1, LANES), 1)
                query = jnp.where(
                    lane < HEADS * MAIN, lane % MAIN, MAIN + (lane - HEADS * MAIN) % REST
                )
                key_row = (key // WLON) % WLAT
                query_row = (query // WLON) % WLAT
                last = at_ref[0] == 7
                same = (key_row < SLAT) == (query_row < SLAT)
                lat_rows = valid_ref.shape[0]
                valid_rows = jnp.concatenate(
                    [valid_ref[lat_rows - SLAT :, :], valid_ref[:SLAT, :]], axis=0
                ).astype(F32)
                row_pick = (
                    key_row == lax.broadcasted_iota(jnp.int32, (WIN, WLAT), 1)
                ).astype(F32)
                key_valid = nn(row_pick, valid_rows)
                column = lax.broadcasted_iota(jnp.int32, (WIN, valid_ref.shape[1]), 1)
                for w in range(2):
                    wanted = at_ref[1] * (2 * WLON) + SLON + WLON * w + key % WLON
                    wanted = jnp.where(wanted >= valid_ref.shape[1], wanted - valid_ref.shape[1], wanted)
                    is_valid = (
                        jnp.sum(jnp.where(column == wanted, key_valid, 0.0), axis=1, keepdims=True)
                        > 0.5
                    )
                    allowed = jnp.logical_and(same, is_valid) | jnp.logical_not(last)
                    bias_t[1 + w] = jnp.where(allowed, wide, NEGATIVE)

    gain = gain_ref[...]
    eye = eye_ref[...]
    lane_head = lax.broadcasted_iota(jnp.int32, (1, features), 1) // HEAD_DIM
    head_masks = [(lane_head == h).astype(F32).astype(BF16) for h in range(HEADS)]
    for b in range(2):
        for n, (own, east, south, corner) in enumerate(
            (
                (fields_ref, east_f_ref, south_f_ref, corner_f_ref),
                (cot_ref, east_c_ref, south_c_ref, corner_c_ref),
            )
        ):
            wide = 2 * WLON
            if b == 0:
                tile[n, :, :, :wide] = own[:, SLAT : SLAT + WLAT]
                tile[n, :, :, wide : wide + SLON] = east[:, SLAT : SLAT + WLAT]
            else:
                tile[n, :, :SLAT, :wide] = own[:, SLAT + WLAT :]
                tile[n, :, :SLAT, wide : wide + SLON] = east[:, SLAT + WLAT :]
                tile[n, :, SLAT:, :wide] = south[...]
                tile[n, :, SLAT:, wide : wide + SLON] = corner[...]
        flat_f = tile[0].reshape(-1, features)
        flat_c = tile[1].reshape(-1, features)
        proj_tile = None
        grads = []
        bias_grad = None
        for w in range(2):
            pick = pick_ref[w]
            x = nn(pick, flat_f)
            cot = nn(pick, flat_c).astype(BF16)
            mean = jnp.mean(x, axis=1, keepdims=True)
            centered = x - mean
            variance = jnp.mean(centered * centered, axis=1, keepdims=True)
            inverse = lax.rsqrt(variance + EPSILON)
            hat = centered * inverse
            normed = (hat * gain).astype(BF16)
            queries = nn(normed, weights[0]).astype(BF16)
            keys = nn(normed, weights[1]).astype(BF16)
            values = nn(normed, weights[2]).astype(BF16)
            keys_t = nt(weights[3], normed).astype(BF16)
            values_t = nt(weights[4], normed).astype(BF16)
            grad_att = nt(cot, proj_ref[...]).astype(BF16)
            q_blocks = head_blocks(queries, head_masks)
            g_blocks = head_blocks(grad_att, head_masks)
            scores = nt(keys, q_blocks) * (SCALE * LOG2E) + bias_t[b * (1 + w)]
            exponent = jnp.exp2(scores - jnp.max(scores, axis=0, keepdims=True))
            soft = exponent * (1.0 / jnp.sum(exponent, axis=0, keepdims=True))
            soft_bf = soft.astype(BF16)
            grad_soft = nt(values, g_blocks)
            delta = jnp.sum(soft * grad_soft, axis=0, keepdims=True)
            grad_scores = soft * (grad_soft - delta)
            bias_grad = grad_scores if bias_grad is None else bias_grad + grad_scores
            grad_bf = grad_scores.astype(BF16)
            grad_values = nn(soft_bf, g_blocks).astype(BF16)
            grad_keys = (nn(grad_bf, q_blocks) * SCALE).astype(BF16)
            attended_t = own_heads(nn(values_t, soft_bf)).astype(BF16)
            grad_queries_t = (own_heads(nn(keys_t, grad_bf)) * SCALE).astype(BF16)
            projected_t = nn(weights[5], attended_t).astype(BF16)
            grad_queries = nt(eye[:WIN, :WIN], grad_queries_t).astype(BF16)
            part = nt(unpick_ref[w], projected_t)
            proj_tile = part if proj_tile is None else proj_tile + part
            grad_normed = (
                nt(grad_queries, weights[0]) + nt(grad_keys, weights[1]) + nt(grad_values, weights[2])
            )
            grad_hat = grad_normed * gain
            grad_x = inverse * (
                grad_hat
                - jnp.mean(grad_hat, axis=1, keepdims=True)
                - hat * jnp.mean(grad_hat * hat, axis=1, keepdims=True)
            )
            grads.append(grad_x.astype(BF16))
        bias_sum[b] += bias_grad
        grad_tile = nn(unpick_ref[0], grads[0]) + nn(unpick_ref[1], grads[1])
        proj_out_ref[:, b] = proj_tile.astype(BF16).reshape(WZ, WLAT, 16, features)
        grad_out_ref[:, b] = grad_tile.astype(BF16).reshape(WZ, WLAT, 16, features)

    @pl.when(step == pl.num_programs(0) - 1)
    def finish():
        for b in range(2):
            rows = nt(bias_pick_ref[...], bias_sum[b].astype(BF16)).astype(BF16)
            bias_out_ref[:, b] = rows.reshape(-1, ROWS, WIN)


def attend(at, fields, cotangent, halos, gain, qkv_weight, proj_weight, bias, valid_mask, parts):
    levels, lat_cells, lon_cells, features = fields.shape
    picks = window_picks()
    constants = (
        jnp.asarray(picks, BF16),
        jnp.asarray(picks.transpose(0, 2, 1), BF16),
        jnp.asarray(bias_picks(parts), BF16),
        jnp.asarray(np.eye(features), BF16),
    )

    def by_level(array):
        return pl.BlockSpec((WZ,) + array.shape[1:], lambda g: (g,) + (0,) * (array.ndim - 1))

    def whole(array):
        return pl.BlockSpec(array.shape, lambda g: (0,) * array.ndim)

    tiled = (fields, cotangent) + tuple(halos)
    fixed = (gain, qkv_weight, proj_weight, bias, valid_mask) + constants
    out_tile = jax.ShapeDtypeStruct((levels, 2, WLAT, 16, features), BF16)
    bias_out = jax.ShapeDtypeStruct(bias.shape, BF16)
    return pl.pallas_call(
        kernel,
        grid=(levels // WZ,),
        out_shape=(out_tile, out_tile, bias_out),
        in_specs=[pl.BlockSpec(memory_space=pltpu.SMEM)]
        + [by_level(a) for a in tiled]
        + [whole(a) for a in fixed],
        out_specs=(by_level(out_tile), by_level(out_tile), whole(bias_out)),
        scratch_shapes=[
            pltpu.VMEM((6, features, features), BF16),
            pltpu.VMEM((3, WIN, LANES), F32),
            pltpu.VMEM((2, WIN, LANES), F32),
            pltpu.VMEM((2, WZ, WLAT, 16, features), BF16),
        ],
        compiler_params=pltpu.CompilerParams(vmem_limit_bytes=48 * 1024 * 1024),
    )(at, *tiled, *fixed)


def shift(block, lat_step, lon_step):
    lats, lons = lax.axis_size("lat"), lax.axis_size("lon")
    route = [
        (((a + lat_step) % lats) * lons + (o + lon_step) % lons, a * lons + o)
        for a in range(lats)
        for o in range(lons)
    ]
    return lax.ppermute(block, ("lat", "lon"), route)


def local(
    fields, cotangent, norm_gain, qkv_weight, proj_weight, bias_table, window_types, valid_mask
):
    levels, lat_cells, lon_cells, features = fields.shape
    lat_at = lax.axis_index("lat")
    lon_at = lax.axis_index("lon")
    parts = lax.axis_size("lon")
    per = WIN // parts
    east = [shift(a[:, :, :SLON], 0, 1) for a in (fields, cotangent)]
    south = [shift(a[:, :SLAT], 1, 0) for a in (fields, cotangent)]
    corner = [shift(a[:, :SLAT, :SLON], 1, 1) for a in (fields, cotangent)]
    my_types = lax.dynamic_slice_in_dim(window_types, lat_at * 2, 2)
    mine = jnp.stack(
        [lax.dynamic_index_in_dim(bias_table, my_types[b], 0, keepdims=False) for b in range(2)]
    ).reshape(2, HEADS * per, WIN)
    mine = jnp.pad(mine, ((0, 0), (0, ROWS - HEADS * per), (0, 0)))
    bias = lax.all_gather(mine, "lon")
    at = jnp.stack([lat_at, lon_at]).astype(jnp.int32)
    proj_buffer, grad_buffer, bias_parts = attend(
        at,
        fields,
        cotangent,
        east + south + corner,
        norm_gain.reshape(1, -1),
        qkv_weight,
        proj_weight,
        bias,
        valid_mask,
        parts,
    )
    bias_mine = lax.all_to_all(bias_parts, "lon", 0, 0, tiled=True)
    grad_bias = jnp.sum(bias_mine.astype(F32), axis=0)[:, : HEADS * per].reshape(
        2, HEADS, per, WIN
    )

    def bring_back(wide, base):
        wide = wide.reshape(levels, lat_cells, 16, features)
        inside = lat_cells - SLAT
        beyond = lon_cells + SLON
        west = shift(wide[:, :inside, lon_cells:beyond], 0, -1)
        north = shift(wide[:, inside:, SLON:lon_cells], -1, 0)
        corner = shift(wide[:, inside:, lon_cells:beyond], -1, -1)
        top = jnp.concatenate([corner, north], axis=2)
        rest = jnp.concatenate([west, wide[:, :inside, SLON:lon_cells]], axis=2)
        own = jnp.concatenate([top, rest], axis=1)
        return (base.astype(F32) + own.astype(F32)).astype(BF16)

    return bring_back(proj_buffer, fields), bring_back(grad_buffer, cotangent), grad_bias


def solution(mesh):
    in_specs = (
        P(None, "lat", "lon", None),
        P(None, "lat", "lon", None),
        P(),
        P(),
        P(),
        P(None, None, "lon", None),
        P(),
        P(),
    )
    out_specs = (
        P(None, "lat", "lon", None),
        P(None, "lat", "lon", None),
        P("lat", None, "lon", None),
    )
    return jax.shard_map(local, mesh=mesh, in_specs=in_specs, out_specs=out_specs, check_vma=False)
```

```python
import functools

import jax
import jax.numpy as jnp
import numpy as np
from jax import lax
from jax.experimental import pallas as pl
from jax.experimental.pallas import tpu as pltpu
from jax.sharding import PartitionSpec as P

HEADS = 6
WZ = 2
WLAT = 12
WLON = 6
WIN = 144
SLAT = 6
SLON = 3
HEAD_DIM = 32
MAIN = 128
REST = WIN - MAIN
LANES = 896
ROWS = 64

NEGATIVE = -1e30
EPSILON = 1e-05
LOG2E = 1.4426950408889634
SCALE = float(HEAD_DIM) ** (-0.5)

F32 = jnp.float32
BF16 = jnp.bfloat16


def nn(a, b):
    return lax.dot_general(a, b, (((1,), (0,)), ((), ())), preferred_element_type=F32)


def nt(a, b):
    return lax.dot_general(a, b, (((1,), (1,)), ((), ())), preferred_element_type=F32)


def tn(a, b):
    return lax.dot_general(a, b, (((0,), (0,)), ((), ())), preferred_element_type=F32)


def lane_of(head, query):
    return np.where(query < MAIN, head * MAIN + query, HEADS * MAIN + head * REST + query - MAIN)


COLS = 2 * WLON
LATS = 2 * WLAT
PAIR = WZ * COLS * LATS
STRIP = 112
CORNER = 48


def tokens(columns, rows):
    return [(z, c, r) for z in range(WZ) for c in columns for r in rows]


def window(b, w):
    return [
        (z, SLON + WLON * w + c, SLAT + WLAT * b + r)
        for z in range(WZ)
        for r in range(WLAT)
        for c in range(WLON)
    ]


def pick(wanted, sources):
    where, at = {}, 0
    for source, length in sources:
        for n, token in enumerate(source):
            where.setdefault(token, at + n)
        at += length
    out = np.zeros((len(wanted), at), np.float32)
    for n, token in enumerate(wanted):
        if token in where:
            out[n, where[token]] = 1
    return out


def padded(rows, length):
    return np.pad(rows, ((0, length - rows.shape[0]), (0, 0)))


OWN_WEST = tokens(range(SLON, SLON + WLON), range(LATS))
OWN_EAST = tokens(range(SLON + WLON, COLS), range(LATS))
EAST = tokens(range(COLS, COLS + SLON), range(SLAT, LATS))
SOUTH = tokens(range(SLON, COLS), range(LATS, LATS + SLAT))
FAR = tokens(range(COLS, COLS + SLON), range(LATS, LATS + SLAT))


def sources_of(b, w):
    if w == 0:
        parts = [(OWN_WEST, len(OWN_WEST))]
    else:
        parts = [(OWN_EAST, len(OWN_EAST)), (EAST, STRIP)]
    if b == 1:
        parts.append((SOUTH, STRIP))
        if w == 1:
            parts.append((FAR, CORNER))
    return parts


def send_picks():
    own = [(tokens(range(COLS), range(LATS)), PAIR)]
    west = pick(tokens(range(SLON), range(SLAT, LATS)), own)
    north = pick(tokens(range(SLON, COLS), range(SLAT)), own)
    corner = pick(tokens(range(SLON), range(SLAT)), own)
    return np.concatenate([padded(west, STRIP), padded(north, STRIP), padded(corner, CORNER)])


def land_picks():
    places = tokens(range(COLS), range(LATS))
    sources = [
        (tokens(range(SLON), range(SLAT, LATS)), STRIP),
        (tokens(range(SLON, COLS), range(SLAT)), STRIP),
        (tokens(range(SLON), range(SLAT)), CORNER),
    ]
    return pick(places, sources)


def bias_picks(parts):
    per = WIN // parts
    pick = np.zeros((parts, ROWS, LANES), np.float32)
    for k in range(parts):
        for h in range(HEADS):
            for r in range(per):
                pick[k, h * per + r, lane_of(h, k * per + r)] = 1
    return pick.reshape(parts * ROWS, LANES)


def head_blocks(tokens, head_masks):
    pieces = [tokens[:MAIN] * head_masks[h] for h in range(HEADS)]
    pieces += [tokens[MAIN:] * head_masks[h] for h in range(HEADS)]
    pieces.append(jnp.zeros((LANES - HEADS * WIN, tokens.shape[1]), tokens.dtype))
    return jnp.concatenate(pieces, axis=0)


def own_heads(wide):
    main, rest = [], []
    for h in range(HEADS):
        rows = wide[h * HEAD_DIM : (h + 1) * HEAD_DIM]
        main.append(rows[:, h * MAIN : (h + 1) * MAIN])
        left = HEADS * MAIN + h * REST
        rest.append(rows[:, left : left + REST])
    return jnp.concatenate(
        [jnp.concatenate(main, axis=0), jnp.concatenate(rest, axis=0)], axis=1
    )


def pack(rows_a, rows_b):
    return jnp.concatenate(
        [
            rows_a[:, :MAIN],
            rows_b[:, :MAIN],
            jnp.concatenate([rows_a[:, MAIN:], rows_b[:, MAIN:]], axis=1),
        ],
        axis=0,
    ).astype(BF16)


def unpack(packed):
    count = packed.shape[0] // 3
    half = packed.shape[1] // 2
    last = packed[2 * count :]
    return (
        jnp.concatenate([packed[:count], last[:, :half]], axis=1),
        jnp.concatenate([packed[count : 2 * count], last[:, half:]], axis=1),
    )


def pack_kernel(
    types_ref, fields_ref, cot_ref, table_ref, pick_ref, eye_ref, east_ref, south_ref, far_ref, mine_ref
):
    features = fields_ref.shape[-1]
    rows = [
        nn(pick_ref[...], ref[...].reshape(-1, features)) for ref in (fields_ref, cot_ref)
    ]
    at = 0
    for ref, count in ((east_ref, STRIP), (south_ref, STRIP), (far_ref, CORNER)):
        ref[0] = pack(*(r[at : at + count] for r in rows))
        at += count

    @pl.when(pl.program_id(0) == 0)
    def choose_bias():
        table = table_ref[...].astype(F32)
        kind = lax.broadcasted_iota(jnp.int32, (1, table.shape[1], 1), 1)
        chosen = []
        for b in range(2):
            one = jnp.sum(jnp.where(kind == types_ref[b], table, 0.0), axis=1)
            chosen.append(one.astype(BF16))
            chosen.append(jnp.zeros((ROWS - one.shape[0], WIN), BF16))
        mine_ref[...] = nt(eye_ref[...], jnp.concatenate(chosen, axis=0)).astype(BF16)


def prepare(b, at_ref, qkv_ref, proj_ref, bias_ref, valid_ref, bias_pick_ref, eye, weights, bias_t):
    features = proj_ref.shape[0]
    for n in range(3):
        weights[n] = qkv_ref[:, n * features : (n + 1) * features]
    weights[3] = nt(eye, weights[1]).astype(BF16)
    weights[4] = nt(eye, weights[2]).astype(BF16)
    weights[5] = nt(eye, proj_ref[...]).astype(BF16)
    table = jnp.concatenate(
        [bias_ref[k, :, b * ROWS : (b + 1) * ROWS] for k in range(bias_ref.shape[0])], axis=1
    )
    wide = nn(table, bias_pick_ref[...]) * LOG2E
    if b == 0:
        bias_t[0] = wide
        return
    key = lax.broadcasted_iota(jnp.int32, (WIN, 1), 0)
    lane = lax.broadcasted_iota(jnp.int32, (1, LANES), 1)
    query = jnp.where(lane < HEADS * MAIN, lane % MAIN, MAIN + (lane - HEADS * MAIN) % REST)
    key_row = (key // WLON) % WLAT
    query_row = (query // WLON) % WLAT
    last = at_ref[0] == at_ref[2] - 1
    same = (key_row < SLAT) == (query_row < SLAT)
    lat_rows, lon_columns = valid_ref.shape
    valid_rows = jnp.concatenate(
        [valid_ref[lat_rows - SLAT :, :], valid_ref[:SLAT, :]], axis=0
    ).astype(F32)
    row_pick = (key_row == lax.broadcasted_iota(jnp.int32, (WIN, WLAT), 1)).astype(F32)
    key_valid = nn(row_pick, valid_rows)
    column = lax.broadcasted_iota(jnp.int32, (WIN, lon_columns), 1)
    for w in range(2):
        wanted = at_ref[1] * COLS + SLON + WLON * w + key % WLON
        wanted = jnp.where(wanted >= lon_columns, wanted - lon_columns, wanted)
        is_valid = (
            jnp.sum(jnp.where(column == wanted, key_valid, 0.0), axis=1, keepdims=True) > 0.5
        )
        allowed = jnp.logical_and(same, is_valid) | jnp.logical_not(last)
        bias_t[w] = jnp.where(allowed, wide, NEGATIVE)


def one_window(flat_f, flat_c, chosen, gain, proj_weight, weights, bias, eye, head_masks):
    x = nn(chosen, flat_f)
    cot = nn(chosen, flat_c).astype(BF16)
    mean = jnp.mean(x, axis=1, keepdims=True)
    centered = x - mean
    variance = jnp.mean(centered * centered, axis=1, keepdims=True)
    inverse = lax.rsqrt(variance + EPSILON)
    hat = centered * inverse
    normed = (hat * gain).astype(BF16)
    queries = nn(normed, weights[0]).astype(BF16)
    keys = nn(normed, weights[1]).astype(BF16)
    values = nn(normed, weights[2]).astype(BF16)
    keys_t = nt(weights[3], normed).astype(BF16)
    values_t = nt(weights[4], normed).astype(BF16)
    grad_att = nt(cot, proj_weight).astype(BF16)
    q_blocks = head_blocks(queries, head_masks)
    g_blocks = head_blocks(grad_att, head_masks)
    scores = nt(keys, q_blocks) * (SCALE * LOG2E) + bias
    exponent = jnp.exp2(scores - jnp.max(scores, axis=0, keepdims=True))
    soft = exponent * (1.0 / jnp.sum(exponent, axis=0, keepdims=True))
    soft_bf = soft.astype(BF16)
    grad_soft = nt(values, g_blocks)
    delta = jnp.sum(soft * grad_soft, axis=0, keepdims=True)
    grad_scores = soft * (grad_soft - delta)
    grad_bf = grad_scores.astype(BF16)
    grad_values = nn(soft_bf, g_blocks).astype(BF16)
    grad_keys = (nn(grad_bf, q_blocks) * SCALE).astype(BF16)
    attended_t = own_heads(nn(values_t, soft_bf)).astype(BF16)
    grad_queries_t = (own_heads(nn(keys_t, grad_bf)) * SCALE).astype(BF16)
    projected_t = nn(weights[5], attended_t).astype(BF16)
    projected = nt(eye[:WIN, :WIN], projected_t).astype(BF16)
    grad_queries = nt(eye[:WIN, :WIN], grad_queries_t).astype(BF16)
    grad_normed = (
        nt(grad_queries, weights[0]) + nt(grad_keys, weights[1]) + nt(grad_values, weights[2])
    )
    grad_hat = grad_normed * gain
    grad_x = inverse * (
        grad_hat
        - jnp.mean(grad_hat, axis=1, keepdims=True)
        - hat * jnp.mean(grad_hat * hat, axis=1, keepdims=True)
    )
    return projected, grad_x.astype(BF16), grad_scores


def attend_kernel(b, *refs):
    (at_ref, fields_ref, cot_ref, east_ref), refs = refs[:4], refs[4:]
    if b == 1:
        (south_ref, far_ref), refs = refs[:2], refs[2:]
    else:
        (before_p_ref, before_g_ref), refs = refs[:2], refs[2:]
    (gain_ref, qkv_ref, proj_ref, bias_ref, valid_ref, bias_pick_ref, eye_ref), refs = (
        refs[:7],
        refs[7:],
    )
    (pick_w_ref, pick_e_ref, place_ref), refs = refs[:3], refs[3:]
    if b == 1:
        (win_p_ref, win_g_ref, strip_ref, bias_out_ref), refs = refs[:4], refs[4:]
    else:
        (mixed_ref, grad_ref, strip_ref, bias_out_ref), refs = refs[:4], refs[4:]
    weights, bias_t, bias_sum = refs
    step = pl.program_id(0)
    features = fields_ref.shape[-1]
    eye = eye_ref[...]

    @pl.when(step == 0)
    def start():
        bias_sum[...] = jnp.zeros_like(bias_sum)
        prepare(
            b, at_ref, qkv_ref, proj_ref, bias_ref, valid_ref, bias_pick_ref, eye, weights, bias_t
        )

    gain = gain_ref[...]
    lane_head = lax.broadcasted_iota(jnp.int32, (1, features), 1) // HEAD_DIM
    head_masks = [(lane_head == h).astype(F32).astype(BF16) for h in range(HEADS)]
    flats = [[], []]
    halo = unpack(east_ref[0])
    if b == 1:
        south, far = unpack(south_ref[0]), unpack(far_ref[0])
    for n, ref in enumerate((fields_ref, cot_ref)):
        west = [ref[:, SLON : SLON + WLON].reshape(-1, features)]
        right = [ref[:, SLON + WLON :].reshape(-1, features), halo[n]]
        if b == 1:
            west.append(south[n])
            right += [south[n], far[n]]
        flats[0].append(jnp.concatenate(west, axis=0))
        flats[1].append(jnp.concatenate(right, axis=0))
    done = [
        one_window(
            *flats[w],
            (pick_w_ref, pick_e_ref)[w][...],
            gain,
            proj_ref[...],
            weights,
            bias_t[w * b],
            eye,
            head_masks,
        )
        for w in range(2)
    ]
    bias_sum[...] += done[0][2] + done[1][2]
    if b == 1:
        placed = []
        for n, ref in enumerate((win_p_ref, win_g_ref)):
            both = jnp.concatenate([done[0][n], done[1][n]], axis=0)
            ref[0] = both
            placed.append(nn(place_ref[...], both))
        strip_ref[0, : 3 * STRIP] = pack(*(p[:STRIP] for p in placed))
        strip_ref[0, 3 * STRIP :] = pack(*(p[STRIP:] for p in placed))
    else:
        placed = []
        for n, (ref, base, out) in enumerate(
            ((before_p_ref, fields_ref, mixed_ref), (before_g_ref, cot_ref, grad_ref))
        ):
            both = jnp.concatenate([done[0][n], done[1][n], ref[0]], axis=0)
            part = nn(place_ref[...], both)
            placed.append(part)
            inner = part[STRIP:].reshape(WZ, COLS - SLON, LATS, features)
            out[:, :SLON] = base[:, :SLON]
            out[:, SLON:] = (base[:, SLON:].astype(F32) + inner).astype(BF16)
        strip_ref[0] = pack(*(p[:STRIP] for p in placed))

    @pl.when(step == pl.num_programs(0) - 1)
    def finish():
        wide = nt(bias_sum[...].astype(BF16), bias_pick_ref[...])
        top, low = wide[:80], wide[80:]
        for k in range(bias_out_ref.shape[0]):
            left = top[:, k * ROWS : (k + 1) * ROWS]
            right = low[:, k * ROWS : (k + 1) * ROWS]
            right = jnp.concatenate([right, jnp.zeros((160 - WIN, ROWS), F32)], axis=0)
            bias_out_ref[k] = jnp.concatenate([left, right], axis=1).astype(BF16)


def land_kernel(
    mixed_ref, grad_ref, west_ref, north_ref, far_ref, bias0_ref, bias1_ref, place_ref,
    out_m_ref, out_g_ref, out_b_ref
):
    features = mixed_ref.shape[-1]
    pieces = [unpack(p) for p in (west_ref[0], north_ref[0, : 3 * STRIP], far_ref[0])]
    for n, (base, out) in enumerate(((mixed_ref, out_m_ref), (grad_ref, out_g_ref))):
        part = nn(place_ref[...], jnp.concatenate([p[n] for p in pieces], axis=0))
        out[...] = (base[...].astype(F32) + part.reshape(base.shape)).astype(BF16)

    @pl.when(pl.program_id(0) == 0)
    def bias():
        count = out_b_ref.shape[0]
        for b, ref in enumerate((bias0_ref, bias1_ref)):
            total = ref[0].astype(F32)
            for k in range(1, ref.shape[0]):
                total = total + ref[k].astype(F32)
            turned = total.T
            whole = jnp.concatenate([turned[:ROWS], turned[ROWS:, : WIN - 80]], axis=1)
            out_b_ref[:, b, :] = whole[:count]


def by_pair(array, size=1):
    return pl.BlockSpec((size,) + array.shape[1:], lambda g: (g,) + (0,) * (array.ndim - 1))


def whole(array):
    return pl.BlockSpec(array.shape, lambda g: (0,) * array.ndim)


def shape_of(*dims, kind=BF16):
    return jax.ShapeDtypeStruct(dims, kind)


def call(body, name, steps, inputs, outputs, scratch=(), flops=10**9):
    in_specs = [spec for _, spec in inputs]
    bytes_moved = sum(a.size * a.dtype.itemsize for a, _ in inputs) + sum(
        int(np.prod(a.shape)) * a.dtype.itemsize for a, _ in outputs
    )
    return pl.pallas_call(
        body,
        name=name,
        grid=(steps,),
        out_shape=tuple(a for a, _ in outputs),
        in_specs=in_specs,
        out_specs=tuple(spec for _, spec in outputs),
        scratch_shapes=list(scratch),
        compiler_params=pltpu.CompilerParams(vmem_limit_bytes=64 * 1024 * 1024),
        cost_estimate=pl.CostEstimate(
            flops=flops, bytes_accessed=bytes_moved, transcendentals=0
        ),
    )(*(a for a, _ in inputs))


def paired(array, size=1):
    return (array, by_pair(array, size))


def entire(array):
    return (array, whole(array))


def in_smem(array):
    return (array, pl.BlockSpec(memory_space=pltpu.SMEM))


def shift(block, lat_step, lon_step):
    lats, lons = lax.axis_size("lat"), lax.axis_size("lon")
    route = [
        (((a + lat_step) % lats) * lons + (o + lon_step) % lons, a * lons + o)
        for a in range(lats)
        for o in range(lons)
    ]
    return lax.ppermute(block, ("lat", "lon"), route)


def local(
    fields, cotangent, norm_gain, qkv_weight, proj_weight, bias_table, window_types, valid_mask
):
    fields = fields.transpose(0, 2, 1, 3)
    cotangent = cotangent.transpose(0, 2, 1, 3)
    levels, lon_cells, lat_cells, features = fields.shape
    lat_at = lax.axis_index("lat")
    lon_at = lax.axis_index("lon")
    parts = lax.axis_size("lon")
    per = WIN // parts
    pairs = levels // WZ
    at = jnp.stack([lat_at, lon_at, lax.axis_size("lat")]).astype(jnp.int32)
    my_types = lax.dynamic_slice_in_dim(window_types, lat_at * 2, 2)
    eye = jnp.asarray(np.eye(features), BF16)
    bias_pick = jnp.asarray(bias_picks(parts), BF16)
    strip = shape_of(pairs, 3 * STRIP, MAIN)
    corner = shape_of(pairs, 3 * CORNER, MAIN)
    both_strips = shape_of(pairs, 3 * (STRIP + CORNER), MAIN)

    table = bias_table.transpose(1, 2, 0, 3).reshape(HEADS * per, -1, WIN)
    send = jnp.asarray(send_picks(), BF16)
    east, south, far, mine = call(
        pack_kernel,
        "pack",
        pairs,
        [
            in_smem(my_types),
            paired(fields, WZ),
            paired(cotangent, WZ),
            entire(table),
            entire(send),
            entire(jnp.asarray(np.eye(WIN), BF16)),
        ],
        [paired(strip), paired(strip), paired(corner), entire(shape_of(WIN, 2 * ROWS))],
    )
    south = shift(south, 1, 0)
    far = shift(far, 1, 1)
    east = shift(east, 0, 1)
    bias = lax.all_to_all(
        jnp.broadcast_to(mine[None], (parts,) + mine.shape), "lon", 0, 0, tiled=True
    )

    shared = [
        entire(a)
        for a in (norm_gain.reshape(1, -1), qkv_weight, proj_weight, bias, valid_mask, bias_pick, eye)
    ]
    bias_block = shape_of(parts, 80, 2 * ROWS)
    window_pair = shape_of(pairs, 2 * WIN, features)

    def scratch(tables):
        return (
            pltpu.VMEM((6, features, features), BF16),
            pltpu.VMEM((tables, WIN, LANES), F32),
            pltpu.VMEM((WIN, LANES), F32),
        )

    def window_picks(b):
        return [
            entire(jnp.asarray(pick(window(b, w), sources_of(b, w)), BF16)) for w in range(2)
        ]

    b_order = [(window(1, 0) + window(1, 1), 2 * WIN)]
    place_b = np.concatenate(
        [padded(pick(SOUTH, b_order), STRIP), padded(pick(FAR, b_order), CORNER)]
    )
    win_p, win_g, north, bias_part1 = call(
        functools.partial(attend_kernel, 1),
        "attend_south",
        pairs,
        [in_smem(at), paired(fields, WZ), paired(cotangent, WZ), paired(east), paired(south), paired(far)]
        + shared
        + window_picks(1)
        + [entire(jnp.asarray(place_b, BF16))],
        [paired(window_pair), paired(window_pair), paired(both_strips), entire(bias_block)],
        scratch(2),
        10**10,
    )
    north = shift(north, -1, 0)
    bias_part1 = lax.all_to_all(bias_part1, "lon", 0, 0, tiled=True)

    all_order = [(window(0, 0) + window(0, 1) + window(1, 0) + window(1, 1), 4 * WIN)]
    place_a = np.concatenate(
        [
            padded(pick(EAST, all_order), STRIP),
            pick(tokens(range(SLON, COLS), range(LATS)), all_order),
        ]
    )
    mixed, grad, west, bias_part0 = call(
        functools.partial(attend_kernel, 0),
        "attend_own",
        pairs,
        [in_smem(at), paired(fields, WZ), paired(cotangent, WZ), paired(east), paired(win_p), paired(win_g)]
        + shared
        + window_picks(0)
        + [entire(jnp.asarray(place_a, BF16))],
        [paired(fields, WZ), paired(cotangent, WZ), paired(strip), entire(bias_block)],
        scratch(1),
        10**10,
    )
    west = shift(west, 0, -1)
    far_back = shift(north[:, 3 * STRIP :], 0, -1)
    bias_part0 = lax.all_to_all(bias_part0, "lon", 0, 0, tiled=True)

    out_bias = shape_of(HEADS * per, 2, WIN, kind=F32)
    mixed, grad, grad_bias = call(
        land_kernel,
        "land",
        pairs,
        [
            paired(mixed, WZ),
            paired(grad, WZ),
            paired(west),
            paired(north),
            paired(far_back),
            entire(bias_part0),
            entire(bias_part1),
            entire(jnp.asarray(land_picks(), BF16)),
        ],
        [paired(fields, WZ), paired(cotangent, WZ), entire(out_bias)],
    )
    grad_bias = grad_bias.reshape(HEADS, per, 2, WIN).transpose(2, 0, 1, 3)
    return mixed.transpose(0, 2, 1, 3), grad.transpose(0, 2, 1, 3), grad_bias


def solution(mesh):
    in_specs = (
        P(None, "lat", "lon", None),
        P(None, "lat", "lon", None),
        P(),
        P(),
        P(),
        P(None, None, "lon", None),
        P(),
        P(),
    )
    out_specs = (
        P(None, "lat", "lon", None),
        P(None, "lat", "lon", None),
        P("lat", None, "lon", None),
    )
    return jax.shard_map(local, mesh=mesh, in_specs=in_specs, out_specs=out_specs, check_vma=False)
```

```python
import functools

import jax
import jax.numpy as jnp
import numpy as np
from jax import lax
from jax.experimental import pallas as pl
from jax.experimental.pallas import tpu as pltpu
from jax.sharding import PartitionSpec as P

HEADS = 6
WZ = 2
WLAT = 12
WLON = 6
WIN = 144
SLAT = 6
SLON = 3
HEAD_DIM = 32
MAIN = 128
REST = WIN - MAIN
LANES = 896
ROWS = 64

NEGATIVE = -1e30
EPSILON = 1e-05
LOG2E = 1.4426950408889634
SCALE = float(HEAD_DIM) ** (-0.5)

F32 = jnp.float32
BF16 = jnp.bfloat16


def nn(a, b):
    return lax.dot_general(a, b, (((1,), (0,)), ((), ())), preferred_element_type=F32)


def nt(a, b):
    return lax.dot_general(a, b, (((1,), (1,)), ((), ())), preferred_element_type=F32)


def tn(a, b):
    return lax.dot_general(a, b, (((0,), (0,)), ((), ())), preferred_element_type=F32)


def lane_of(head, query):
    return np.where(query < MAIN, head * MAIN + query, HEADS * MAIN + head * REST + query - MAIN)


COLS = 2 * WLON
LATS = 2 * WLAT
PAIR = WZ * COLS * LATS
STRIP = 112
CORNER = 48


def tokens(columns, rows):
    return [(z, c, r) for z in range(WZ) for c in columns for r in rows]


def window(b, w):
    return [
        (z, SLON + WLON * w + c, SLAT + WLAT * b + r)
        for z in range(WZ)
        for r in range(WLAT)
        for c in range(WLON)
    ]


def pick(wanted, sources):
    where, at = {}, 0
    for source, length in sources:
        for n, token in enumerate(source):
            where.setdefault(token, at + n)
        at += length
    out = np.zeros((len(wanted), at), np.float32)
    for n, token in enumerate(wanted):
        if token in where:
            out[n, where[token]] = 1
    return out


def padded(rows, length):
    return np.pad(rows, ((0, length - rows.shape[0]), (0, 0)))


OWN_WEST = tokens(range(SLON, SLON + WLON), range(LATS))
OWN_EAST = tokens(range(SLON + WLON, COLS), range(LATS))
EAST_COLUMNS = range(COLS, COLS + SLON)
EAST = tokens(EAST_COLUMNS, range(SLAT, LATS))
SOUTH = tokens(range(SLON, COLS), range(LATS, LATS + SLAT))
FAR = tokens(EAST_COLUMNS, range(LATS, LATS + SLAT))


def sources_of(b, w):
    if w == 0:
        parts = [(OWN_WEST, len(OWN_WEST))]
    else:
        parts = [(OWN_EAST, len(OWN_EAST)), (EAST, STRIP)]
    if b == 1:
        parts.append((SOUTH, STRIP))
        if w == 1:
            parts.append((FAR, CORNER))
    return parts


def send_picks():
    own = [(tokens(range(COLS), range(LATS)), PAIR)]
    west = pick(tokens(range(SLON), range(SLAT, LATS)), own)
    north = pick(tokens(range(SLON, COLS), range(SLAT)), own)
    corner = pick(tokens(range(SLON), range(SLAT)), own)
    return np.concatenate([padded(west, STRIP), padded(north, STRIP), padded(corner, CORNER)])


def land_picks():
    sources = [
        (tokens(range(SLON), range(SLAT, LATS)), STRIP),
        (tokens(range(SLON, COLS), range(SLAT)), STRIP),
        (tokens(range(SLON), range(SLAT)), CORNER),
    ]
    return pick(tokens(range(COLS), range(LATS)), sources)


def bias_picks(parts):
    per = WIN // parts
    pick = np.zeros((parts, ROWS, LANES), np.float32)
    for k in range(parts):
        for h in range(HEADS):
            for r in range(per):
                pick[k, h * per + r, lane_of(h, k * per + r)] = 1
    return pick.reshape(parts * ROWS, LANES)


def head_blocks(tokens, head_masks):
    pieces = [tokens[:MAIN] * head_masks[h] for h in range(HEADS)]
    pieces += [tokens[MAIN:] * head_masks[h] for h in range(HEADS)]
    pieces.append(jnp.zeros((LANES - HEADS * WIN, tokens.shape[1]), tokens.dtype))
    return jnp.concatenate(pieces, axis=0)


def own_heads(wide):
    main, rest = [], []
    for h in range(HEADS):
        rows = wide[h * HEAD_DIM : (h + 1) * HEAD_DIM]
        main.append(rows[:, h * MAIN : (h + 1) * MAIN])
        left = HEADS * MAIN + h * REST
        rest.append(rows[:, left : left + REST])
    return jnp.concatenate(
        [jnp.concatenate(main, axis=0), jnp.concatenate(rest, axis=0)], axis=1
    )


def pack(rows_a, rows_b):
    return jnp.concatenate(
        [
            rows_a[:, :MAIN],
            rows_b[:, :MAIN],
            jnp.concatenate([rows_a[:, MAIN:], rows_b[:, MAIN:]], axis=1),
        ],
        axis=0,
    ).astype(BF16)


def unpack(packed):
    count = packed.shape[0] // 3
    half = packed.shape[1] // 2
    last = packed[2 * count :]
    return (
        jnp.concatenate([packed[:count], last[:, :half]], axis=1),
        jnp.concatenate([packed[count : 2 * count], last[:, half:]], axis=1),
    )


def pack_kernel(
    at_ref,
    types_ref,
    fields_ref,
    cot_ref,
    table_ref,
    pick_ref,
    eye_ref,
    east_ref,
    south_ref,
    far_ref,
    mine_ref,
):
    features = fields_ref.shape[-1]
    table = table_ref[...].astype(F32)
    kind = lax.broadcasted_iota(jnp.int32, (1, table.shape[1], 1), 1)
    chosen = []
    for b in range(2):
        one = jnp.sum(jnp.where(kind == types_ref[2 * at_ref[0] + b], table, 0.0), axis=1)
        chosen.append(one.astype(BF16))
        chosen.append(jnp.zeros((ROWS - one.shape[0], WIN), BF16))
    mine = nt(eye_ref[...], jnp.concatenate(chosen, axis=0)).astype(BF16)
    mine_ref[...] = jnp.broadcast_to(mine[None], mine_ref.shape)
    for g in range(east_ref.shape[0]):
        rows = [
            nn(pick_ref[...], ref[WZ * g : WZ * (g + 1)].reshape(-1, features))
            for ref in (fields_ref, cot_ref)
        ]
        at = 0
        for ref, count in ((east_ref, STRIP), (south_ref, STRIP), (far_ref, CORNER)):
            ref[g] = pack(*(r[at : at + count] for r in rows))
            at += count


def prepare_weights(qkv_ref, proj_ref, eye, weights):
    features = proj_ref.shape[0]
    for n in range(3):
        weights[n] = qkv_ref[:, n * features : (n + 1) * features]
    weights[3] = nt(eye, weights[1]).astype(BF16)
    weights[4] = nt(eye, weights[2]).astype(BF16)
    weights[5] = nt(eye, proj_ref[...]).astype(BF16)


def wide_bias(b, bias_ref, bias_pick_ref):
    table = jnp.concatenate(
        [bias_ref[k, :, b * ROWS : (b + 1) * ROWS] for k in range(bias_ref.shape[0])], axis=1
    )
    return nn(table, bias_pick_ref[...]) * LOG2E


def masked_tables(wide, at_ref, valid_ref, tables):
    key = lax.broadcasted_iota(jnp.int32, (WIN, 1), 0)
    lane = lax.broadcasted_iota(jnp.int32, (1, LANES), 1)
    query = jnp.where(lane < HEADS * MAIN, lane % MAIN, MAIN + (lane - HEADS * MAIN) % REST)
    key_row = (key // WLON) % WLAT
    query_row = (query // WLON) % WLAT
    last = at_ref[0] == at_ref[2] - 1
    same = (key_row < SLAT) == (query_row < SLAT)
    lat_rows, lon_columns = valid_ref.shape
    valid_rows = jnp.concatenate(
        [valid_ref[lat_rows - SLAT :, :], valid_ref[:SLAT, :]], axis=0
    ).astype(F32)
    row_pick = (key_row == lax.broadcasted_iota(jnp.int32, (WIN, WLAT), 1)).astype(F32)
    key_valid = nn(row_pick, valid_rows)
    column = lax.broadcasted_iota(jnp.int32, (WIN, lon_columns), 1)
    for w in range(2):
        wanted = at_ref[1] * COLS + SLON + WLON * w + key % WLON
        wanted = jnp.where(wanted >= lon_columns, wanted - lon_columns, wanted)
        is_valid = (
            jnp.sum(jnp.where(column == wanted, key_valid, 0.0), axis=1, keepdims=True) > 0.5
        )
        allowed = jnp.logical_and(same, is_valid) | jnp.logical_not(last)
        tables[w] = jnp.where(allowed, wide, NEGATIVE)


def one_window(flat_f, flat_c, chosen, gain, proj_weight, weights, bias, eye, head_masks):
    x = nn(chosen, flat_f)
    cot = nn(chosen, flat_c).astype(BF16)
    mean = jnp.mean(x, axis=1, keepdims=True)
    centered = x - mean
    variance = jnp.mean(centered * centered, axis=1, keepdims=True)
    inverse = lax.rsqrt(variance + EPSILON)
    hat = centered * inverse
    normed = (hat * gain).astype(BF16)
    queries = nn(normed, weights[0]).astype(BF16)
    keys = nn(normed, weights[1]).astype(BF16)
    values = nn(normed, weights[2]).astype(BF16)
    keys_t = nt(weights[3], normed).astype(BF16)
    values_t = nt(weights[4], normed).astype(BF16)
    grad_att = nt(cot, proj_weight).astype(BF16)
    q_blocks = head_blocks(queries, head_masks)
    g_blocks = head_blocks(grad_att, head_masks)
    scores = nt(keys, q_blocks) * (SCALE * LOG2E) + bias
    exponent = jnp.exp2(scores - jnp.max(scores, axis=0, keepdims=True))
    soft = exponent * (1.0 / jnp.sum(exponent, axis=0, keepdims=True))
    soft_bf = soft.astype(BF16)
    grad_soft = nt(values, g_blocks)
    delta = jnp.sum(soft * grad_soft, axis=0, keepdims=True)
    grad_scores = soft * (grad_soft - delta)
    grad_bf = grad_scores.astype(BF16)
    grad_values = nn(soft_bf, g_blocks).astype(BF16)
    grad_keys = (nn(grad_bf, q_blocks) * SCALE).astype(BF16)
    attended_t = own_heads(nn(values_t, soft_bf)).astype(BF16)
    grad_queries_t = (own_heads(nn(keys_t, grad_bf)) * SCALE).astype(BF16)
    projected_t = nn(weights[5], attended_t).astype(BF16)
    projected = nt(eye[:WIN, :WIN], projected_t).astype(BF16)
    grad_queries = nt(eye[:WIN, :WIN], grad_queries_t).astype(BF16)
    grad_normed = (
        nt(grad_queries, weights[0]) + nt(grad_keys, weights[1]) + nt(grad_values, weights[2])
    )
    grad_hat = grad_normed * gain
    grad_x = inverse * (
        grad_hat
        - jnp.mean(grad_hat, axis=1, keepdims=True)
        - hat * jnp.mean(grad_hat * hat, axis=1, keepdims=True)
    )
    return projected, grad_x.astype(BF16), grad_scores


def run_windows(todo, r, tables, pair):
    features = r["fields"].shape[-1]
    levels = slice(WZ * pair, WZ * (pair + 1))
    lane_head = lax.broadcasted_iota(jnp.int32, (1, features), 1) // HEAD_DIM
    head_masks = [(lane_head == h).astype(F32).astype(BF16) for h in range(HEADS)]
    eye = r["eye"][...]
    halos = {k: unpack(r[k][pair]) for k in ("east", "south", "far") if k in r}
    done, total = [], None
    for b, w in todo:
        flats = []
        for n, ref in enumerate((r["fields"], r["cot"])):
            columns = slice(SLON, SLON + WLON) if w == 0 else slice(SLON + WLON, COLS)
            parts = [ref[levels, columns].reshape(-1, features)]
            if w == 1:
                parts.append(halos["east"][n])
            if b == 1:
                parts.append(halos["south"][n])
                if w == 1:
                    parts.append(halos["far"][n])
            flats.append(jnp.concatenate(parts, axis=0))
        projected, grad, scores = one_window(
            *flats,
            r["pick%d" % w][...],
            r["gain"][...],
            r["proj"][...],
            r["weights"],
            tables(w),
            eye,
            head_masks,
        )
        done.append((projected, grad))
        total = scores if total is None else total + scores
    return done, total


def first_kernel(names, group, *refs):
    r = dict(zip(names, refs))

    @pl.when(pl.program_id(0) == 0)
    def start():
        prepare_weights(r["qkv"], r["proj"], r["eye"][...], r["weights"])
        r["table"][...] = wide_bias(0, r["bias"], r["bias_pick"])
        r["sum"][...] = jnp.zeros_like(r["sum"])

    totals = []
    for pair in range(group):
        done, total = run_windows([(0, 1)], r, lambda w: r["table"][...], pair)
        r["win_p"][pair], r["win_g"][pair] = done[0]
        totals.append(total)
    r["sum"][...] += sum(totals[1:], totals[0])


def south_kernel(names, group, *refs):
    r = dict(zip(names, refs))

    @pl.when(pl.program_id(0) == 0)
    def start():
        wide = wide_bias(1, r["bias"], r["bias_pick"])
        masked_tables(wide, r["at"], r["valid"], r["tables"])
        r["sum"][...] = jnp.zeros_like(r["sum"])

    for pair in range(group):
        done, total = run_windows([(1, 0), (1, 1)], r, lambda w: r["tables"][w], pair)
        r["sum"][...] += total
        placed = []
        for n, (first, out) in enumerate(
            ((r["first_p"], r["win_p"]), (r["first_g"], r["win_g"]))
        ):
            both = jnp.concatenate([done[0][n], done[1][n]], axis=0)
            out[pair] = both
            placed.append(nn(r["place"][...], jnp.concatenate([first[pair], both], axis=0)))
        r["west"][pair] = pack(*(p[:STRIP] for p in placed))
        r["north"][pair] = pack(*(p[STRIP : 2 * STRIP] for p in placed))
        r["corner"][pair] = pack(*(p[2 * STRIP :] for p in placed))


def last_kernel(names, group, *refs):
    r = dict(zip(names, refs))
    step = pl.program_id(0)
    features = r["fields"].shape[-1]

    @pl.when(step == 0)
    def start():
        r["sum"][...] = r["sum0"][...]

    for pair in range(group):
        done, total = run_windows([(0, 0)], r, lambda w: r["table"][...], pair)
        r["sum"][...] += total
        levels = slice(WZ * pair, WZ * (pair + 1))
        for n, (first, south, base, out) in enumerate(
            (
                (r["first_p"], r["south_p"], r["fields"], r["mixed"]),
                (r["first_g"], r["south_g"], r["cot"], r["grad"]),
            )
        ):
            every = jnp.concatenate([done[0][n], first[pair], south[pair]], axis=0)
            part = nn(r["place"][...], every)
            inner = part.reshape(WZ, COLS - SLON, LATS, features)
            out[levels, :SLON] = base[levels, :SLON]
            out[levels, SLON:] = (base[levels, SLON:].astype(F32) + inner).astype(BF16)

    @pl.when(step == pl.num_programs(0) - 1)
    def finish():
        out = r["bias_out"]
        for b, ref in enumerate((r["sum"], r["sum1"])):
            wide = nt(ref[...].astype(BF16), r["bias_pick"][...])
            top, low = wide[:80], wide[80:]
            for k in range(out.shape[0]):
                left = top[:, k * ROWS : (k + 1) * ROWS]
                right = low[:, k * ROWS : (k + 1) * ROWS]
                right = jnp.concatenate([right, jnp.zeros((160 - WIN, ROWS), F32)], axis=0)
                block = jnp.concatenate([left, right], axis=1).astype(BF16)
                out[k, 80 * b : 80 * (b + 1)] = block


def add_strips(strips, base_refs, place_ref, out_refs):
    for pair in range(strips[0].shape[0]):
        pieces = [unpack(ref[pair]) for ref in strips]
        levels = slice(WZ * pair, WZ * (pair + 1))
        for n, (base, out) in enumerate(zip(base_refs, out_refs)):
            own = base[levels]
            part = nn(place_ref[...], jnp.concatenate([p[n] for p in pieces], axis=0))
            out[levels] = (own.astype(F32) + part.reshape(own.shape)).astype(BF16)


def land_kernel(
    mixed_ref, grad_ref, west_ref, north_ref, far_ref, place_ref, out_m_ref, out_g_ref
):
    strips = (west_ref, north_ref, far_ref)
    add_strips(strips, (mixed_ref, grad_ref), place_ref, (out_m_ref, out_g_ref))


def bias_kernel(bias_ref, out_ref):
    count = out_ref.shape[0]
    total = bias_ref[0].astype(F32)
    for k in range(1, bias_ref.shape[0]):
        total = total + bias_ref[k].astype(F32)
    for b in range(2):
        turned = total[80 * b : 80 * (b + 1)].T
        whole = jnp.concatenate([turned[:ROWS], turned[ROWS:, : WIN - 80]], axis=1)
        out_ref[:, b, :] = whole[:count]


def by_pair(array, size=1):
    return pl.BlockSpec((size,) + array.shape[1:], lambda g: (g,) + (0,) * (array.ndim - 1))


def whole(array):
    return pl.BlockSpec(array.shape, lambda g: (0,) * array.ndim)


def shape_of(*dims, kind=BF16):
    return jax.ShapeDtypeStruct(dims, kind)


def call(body, name, steps, inputs, outputs, scratch=(), flops=10**9, aliases=()):
    in_specs = [spec for _, spec in inputs]
    bytes_moved = sum(a.size * a.dtype.itemsize for a, _ in inputs) + sum(
        int(np.prod(a.shape)) * a.dtype.itemsize for a, _ in outputs
    )
    return pl.pallas_call(
        body,
        name=name,
        grid=(steps,),
        out_shape=tuple(a for a, _ in outputs),
        in_specs=in_specs,
        out_specs=tuple(spec for _, spec in outputs),
        scratch_shapes=list(scratch),
        input_output_aliases=dict(aliases),
        compiler_params=pltpu.CompilerParams(vmem_limit_bytes=64 * 1024 * 1024),
        cost_estimate=pl.CostEstimate(
            flops=flops, bytes_accessed=bytes_moved, transcendentals=0
        ),
    )(*(a for a, _ in inputs))


def paired(array, size=1):
    return (array, by_pair(array, size))


def entire(array):
    return (array, whole(array))


def in_smem(array):
    return (array, pl.BlockSpec(memory_space=pltpu.SMEM))


def attend(body, name, steps, inputs, outputs, scratch=()):
    scratch = dict(scratch)
    names = list(inputs) + list(outputs) + list(scratch)
    group = inputs["fields"][1].block_shape[0] // WZ
    results = call(
        functools.partial(body, names, group),
        name,
        steps,
        list(inputs.values()),
        list(outputs.values()),
        list(scratch.values()),
        10**10,
    )
    return dict(zip(outputs, results))


def shift(block, lat_step, lon_step):
    lats, lons = lax.axis_size("lat"), lax.axis_size("lon")
    route = [
        (((a + lat_step) % lats) * lons + (o + lon_step) % lons, a * lons + o)
        for a in range(lats)
        for o in range(lons)
    ]
    return lax.ppermute(block, ("lat", "lon"), route)


def local(
    fields, cotangent, norm_gain, qkv_weight, proj_weight, bias_table, window_types, valid_mask
):
    fields = fields.transpose(0, 2, 1, 3)
    cotangent = cotangent.transpose(0, 2, 1, 3)
    levels, lon_cells, lat_cells, features = fields.shape
    lat_at = lax.axis_index("lat")
    lon_at = lax.axis_index("lon")
    parts = lax.axis_size("lon")
    per = WIN // parts
    pairs = levels // WZ
    at = jnp.stack([lat_at, lon_at, lax.axis_size("lat")]).astype(jnp.int32)
    strip = shape_of(pairs, 3 * STRIP, MAIN)
    corner = shape_of(pairs, 3 * CORNER, MAIN)

    table = bias_table.transpose(1, 2, 0, 3).reshape(HEADS * per, -1, WIN)
    east, south, far, mine = call(
        pack_kernel,
        "pack",
        1,
        [
            in_smem(at),
            in_smem(window_types),
            entire(fields),
            entire(cotangent),
            entire(table),
            entire(jnp.asarray(send_picks(), BF16)),
            entire(jnp.asarray(np.eye(WIN), BF16)),
        ],
        [entire(strip), entire(strip), entire(corner), entire(shape_of(parts, WIN, 2 * ROWS))],
    )
    east = shift(east, 0, 1)
    bias = lax.all_to_all(mine, "lon", 0, 0, tiled=True)
    south, far, bias = lax.optimization_barrier((south, far, bias))
    south = shift(south, 1, 0)
    far = shift(far, 1, 1)

    gain = norm_gain.reshape(1, -1)
    windows = {(b, w): window(b, w) for b in range(2) for w in range(2)}
    steps = 2
    group = pairs // steps

    def constant(rows):
        return entire(jnp.asarray(rows, BF16))

    def split(array):
        return paired(array, group)

    def strip_of(count):
        return split(shape_of(pairs, 3 * count, MAIN))

    def tokens_of(count):
        return split(shape_of(pairs, count, features))

    def picked(b, w):
        return constant(pick(windows[b, w], sources_of(b, w)))

    wide_sum = entire(shape_of(WIN, LANES, kind=F32))
    common = {
        "fields": paired(fields, WZ * group),
        "cot": paired(cotangent, WZ * group),
        "gain": entire(gain),
        "proj": entire(proj_weight),
        "eye": constant(np.eye(features)),
    }
    bias_pick = constant(bias_picks(parts))
    first = attend(
        first_kernel,
        "attend_first",
        steps,
        common
        | {
            "east": split(east),
            "qkv": entire(qkv_weight),
            "bias": entire(bias),
            "bias_pick": bias_pick,
            "pick1": picked(0, 1),
        },
        {
            "win_p": tokens_of(WIN),
            "win_g": tokens_of(WIN),
            "weights": entire(shape_of(6, features, features)),
            "table": wide_sum,
            "sum": wide_sum,
        },
    )
    order = [(windows[0, 1] + windows[1, 0] + windows[1, 1], 3 * WIN)]
    place = [
        padded(pick(EAST, order), STRIP),
        padded(pick(SOUTH, order), STRIP),
        padded(pick(FAR, order), CORNER),
    ]
    below = attend(
        south_kernel,
        "attend_south",
        steps,
        common
        | {
            "at": in_smem(at),
            "east": split(east),
            "south": split(south),
            "far": split(far),
            "first_p": split(first["win_p"]),
            "first_g": split(first["win_g"]),
            "weights": entire(first["weights"]),
            "bias": entire(bias),
            "valid": entire(valid_mask),
            "bias_pick": bias_pick,
            "pick0": picked(1, 0),
            "pick1": picked(1, 1),
            "place": constant(np.concatenate(place)),
        },
        {
            "win_p": tokens_of(2 * WIN),
            "win_g": tokens_of(2 * WIN),
            "west": strip_of(STRIP),
            "north": strip_of(STRIP),
            "corner": strip_of(CORNER),
            "sum": wide_sum,
        },
        {"tables": pltpu.VMEM((2, WIN, LANES), F32)},
    )
    north = shift(below["north"], -1, 0)
    far_back = shift(below["corner"], -1, -1)
    west = shift(below["west"], 0, -1)
    every = [(windows[0, 0] + windows[0, 1] + windows[1, 0] + windows[1, 1], 4 * WIN)]
    place = pick(tokens(range(SLON, COLS), range(LATS)), every)
    last = attend(
        last_kernel,
        "attend_last",
        steps,
        common
        | {
            "first_p": split(first["win_p"]),
            "first_g": split(first["win_g"]),
            "south_p": split(below["win_p"]),
            "south_g": split(below["win_g"]),
            "weights": entire(first["weights"]),
            "table": entire(first["table"]),
            "sum0": entire(first["sum"]),
            "sum1": entire(below["sum"]),
            "bias_pick": bias_pick,
            "pick0": picked(0, 0),
            "place": constant(place),
        },
        {
            "mixed": paired(shape_of(*fields.shape), WZ * group),
            "grad": paired(shape_of(*fields.shape), WZ * group),
            "bias_out": entire(shape_of(parts, 160, 2 * ROWS)),
        },
        {"sum": pltpu.VMEM((WIN, LANES), F32)},
    )
    mixed, grad = last["mixed"], last["grad"]
    bias_sums = lax.all_to_all(last["bias_out"], "lon", 0, 0, tiled=True)

    out_bias = shape_of(HEADS * per, 2, WIN, kind=F32)
    block = paired(shape_of(*fields.shape), WZ * group)
    mixed, grad = call(
        land_kernel,
        "land",
        steps,
        [
            paired(mixed, WZ * group),
            paired(grad, WZ * group),
            split(west),
            split(north),
            split(far_back),
            constant(land_picks()),
        ],
        [block, block],
        flops=10**11,
    )
    (grad_bias,) = call(bias_kernel, "bias_sum", 1, [entire(bias_sums)], [entire(out_bias)])
    grad_bias = grad_bias.reshape(HEADS, per, 2, WIN).transpose(2, 0, 1, 3)
    return mixed.transpose(0, 2, 1, 3), grad.transpose(0, 2, 1, 3), grad_bias


def solution(mesh):
    in_specs = (
        P(None, "lat", "lon", None),
        P(None, "lat", "lon", None),
        P(),
        P(),
        P(),
        P(None, None, "lon", None),
        P(),
        P(),
    )
    out_specs = (
        P(None, "lat", "lon", None),
        P(None, "lat", "lon", None),
        P("lat", None, "lon", None),
    )
    return jax.shard_map(local, mesh=mesh, in_specs=in_specs, out_specs=out_specs, check_vma=False)
```

```python
import functools

import jax
import jax.numpy as jnp
import numpy as np
from jax import lax
from jax.experimental import pallas as pl
from jax.experimental.pallas import tpu as pltpu
from jax.sharding import PartitionSpec as P

HEADS = 6
WZ = 2
WLAT = 12
WLON = 6
WIN = 144
SLAT = 6
SLON = 3
HEAD_DIM = 32
MAIN = 128
REST = WIN - MAIN
LANES = 896
ROWS = 64

NEGATIVE = -1e30
EPSILON = 1e-05
LOG2E = 1.4426950408889634
SCALE = float(HEAD_DIM) ** (-0.5)

F32 = jnp.float32
BF16 = jnp.bfloat16


def nn(a, b):
    return lax.dot_general(a, b, (((1,), (0,)), ((), ())), preferred_element_type=F32)


def nt(a, b):
    return lax.dot_general(a, b, (((1,), (1,)), ((), ())), preferred_element_type=F32)


def tn(a, b):
    return lax.dot_general(a, b, (((0,), (0,)), ((), ())), preferred_element_type=F32)


def lane_of(head, query):
    return np.where(query < MAIN, head * MAIN + query, HEADS * MAIN + head * REST + query - MAIN)


COLS = 2 * WLON
LATS = 2 * WLAT
PAIR = WZ * COLS * LATS
STRIP = 112
CORNER = 48


def tokens(columns, rows):
    return [(z, c, r) for z in range(WZ) for c in columns for r in rows]


def window(b, w):
    return [
        (z, SLON + WLON * w + c, SLAT + WLAT * b + r)
        for z in range(WZ)
        for r in range(WLAT)
        for c in range(WLON)
    ]


def pick(wanted, sources):
    where, at = {}, 0
    for source, length in sources:
        for n, token in enumerate(source):
            where.setdefault(token, at + n)
        at += length
    out = np.zeros((len(wanted), at), np.float32)
    for n, token in enumerate(wanted):
        if token in where:
            out[n, where[token]] = 1
    return out


def padded(rows, length):
    return np.pad(rows, ((0, length - rows.shape[0]), (0, 0)))


OWN_WEST = tokens(range(SLON, SLON + WLON), range(LATS))
OWN_EAST = tokens(range(SLON + WLON, COLS), range(LATS))
EAST_COLUMNS = range(COLS, COLS + SLON)
EAST = tokens(EAST_COLUMNS, range(SLAT, LATS))
SOUTH = tokens(range(SLON, COLS), range(LATS, LATS + SLAT))
FAR = tokens(EAST_COLUMNS, range(LATS, LATS + SLAT))


def sources_of(b, w):
    if w == 0:
        parts = [(OWN_WEST, len(OWN_WEST))]
    else:
        parts = [(OWN_EAST, len(OWN_EAST)), (EAST, STRIP)]
    if b == 1:
        parts.append((SOUTH, STRIP))
        if w == 1:
            parts.append((FAR, CORNER))
    return parts


def send_picks():
    own = [(tokens(range(COLS), range(LATS)), PAIR)]
    west = pick(tokens(range(SLON), range(SLAT, LATS)), own)
    north = pick(tokens(range(SLON, COLS), range(SLAT)), own)
    corner = pick(tokens(range(SLON), range(SLAT)), own)
    return np.concatenate([padded(west, STRIP), padded(north, STRIP), padded(corner, CORNER)])


def land_picks():
    sources = [
        (window(0, 0), WIN),
        (window(0, 1), WIN),
        (window(1, 0) + window(1, 1), 2 * WIN),
        (tokens(range(SLON), range(SLAT, LATS)), STRIP),
        (tokens(range(SLON, COLS), range(SLAT)), STRIP),
        (tokens(range(SLON), range(SLAT)), CORNER),
    ]
    return pick(tokens(range(COLS), range(LATS)), sources)


def bias_picks(parts):
    per = WIN // parts
    pick = np.zeros((parts, ROWS, LANES), np.float32)
    for k in range(parts):
        for h in range(HEADS):
            for r in range(per):
                pick[k, h * per + r, lane_of(h, k * per + r)] = 1
    return pick.reshape(parts * ROWS, LANES)


def head_blocks(tokens, head_masks):
    pieces = [tokens[:MAIN] * head_masks[h] for h in range(HEADS)]
    pieces += [tokens[MAIN:] * head_masks[h] for h in range(HEADS)]
    pieces.append(jnp.zeros((LANES - HEADS * WIN, tokens.shape[1]), tokens.dtype))
    return jnp.concatenate(pieces, axis=0)


def own_heads(wide):
    main, rest = [], []
    for h in range(HEADS):
        rows = wide[h * HEAD_DIM : (h + 1) * HEAD_DIM]
        main.append(rows[:, h * MAIN : (h + 1) * MAIN])
        left = HEADS * MAIN + h * REST
        rest.append(rows[:, left : left + REST])
    return jnp.concatenate(
        [jnp.concatenate(main, axis=0), jnp.concatenate(rest, axis=0)], axis=1
    )


def pack(rows_a, rows_b):
    return jnp.concatenate(
        [
            rows_a[:, :MAIN],
            rows_b[:, :MAIN],
            jnp.concatenate([rows_a[:, MAIN:], rows_b[:, MAIN:]], axis=1),
        ],
        axis=0,
    ).astype(BF16)


def unpack(packed):
    count = packed.shape[0] // 3
    half = packed.shape[1] // 2
    last = packed[2 * count :]
    return (
        jnp.concatenate([packed[:count], last[:, :half]], axis=1),
        jnp.concatenate([packed[count : 2 * count], last[:, half:]], axis=1),
    )


def choose_kernel(at_ref, types_ref, table_ref, eye_ref, mine_ref):
    table = table_ref[...].astype(F32)
    kind = lax.broadcasted_iota(jnp.int32, (1, table.shape[1], 1), 1)
    chosen = []
    for b in range(2):
        one = jnp.sum(jnp.where(kind == types_ref[2 * at_ref[0] + b], table, 0.0), axis=1)
        chosen.append(one.astype(BF16))
        chosen.append(jnp.zeros((ROWS - one.shape[0], WIN), BF16))
    mine = nt(eye_ref[...], jnp.concatenate(chosen, axis=0)).astype(BF16)
    mine_ref[...] = jnp.broadcast_to(mine[None], mine_ref.shape)


def pack_kernel(fields_ref, cot_ref, pick_ref, east_ref, south_ref, far_ref):
    features = fields_ref.shape[-1]
    for g in range(east_ref.shape[0]):
        rows = [
            nn(pick_ref[...], ref[WZ * g : WZ * (g + 1)].reshape(-1, features))
            for ref in (fields_ref, cot_ref)
        ]
        at = 0
        for ref, count in ((east_ref, STRIP), (south_ref, STRIP), (far_ref, CORNER)):
            ref[g] = pack(*(r[at : at + count] for r in rows))
            at += count


def prepare_weights(qkv_ref, proj_ref, eye, weights):
    features = proj_ref.shape[0]
    for n in range(3):
        weights[n] = qkv_ref[:, n * features : (n + 1) * features]
    weights[3] = nt(eye, weights[1]).astype(BF16)
    weights[4] = nt(eye, weights[2]).astype(BF16)
    weights[5] = nt(eye, proj_ref[...]).astype(BF16)


def wide_bias(b, bias_ref, bias_pick_ref):
    table = jnp.concatenate(
        [bias_ref[k, :, b * ROWS : (b + 1) * ROWS] for k in range(bias_ref.shape[0])], axis=1
    )
    return nn(table, bias_pick_ref[...]) * LOG2E


def masked_tables(wide, at_ref, valid_ref, tables):
    key = lax.broadcasted_iota(jnp.int32, (WIN, 1), 0)
    lane = lax.broadcasted_iota(jnp.int32, (1, LANES), 1)
    query = jnp.where(lane < HEADS * MAIN, lane % MAIN, MAIN + (lane - HEADS * MAIN) % REST)
    key_row = (key // WLON) % WLAT
    query_row = (query // WLON) % WLAT
    last = at_ref[0] == at_ref[2] - 1
    same = (key_row < SLAT) == (query_row < SLAT)
    lat_rows, lon_columns = valid_ref.shape
    valid_rows = jnp.concatenate(
        [valid_ref[lat_rows - SLAT :, :], valid_ref[:SLAT, :]], axis=0
    ).astype(F32)
    row_pick = (key_row == lax.broadcasted_iota(jnp.int32, (WIN, WLAT), 1)).astype(F32)
    key_valid = nn(row_pick, valid_rows)
    column = lax.broadcasted_iota(jnp.int32, (WIN, lon_columns), 1)
    for w in range(2):
        wanted = at_ref[1] * COLS + SLON + WLON * w + key % WLON
        wanted = jnp.where(wanted >= lon_columns, wanted - lon_columns, wanted)
        is_valid = (
            jnp.sum(jnp.where(column == wanted, key_valid, 0.0), axis=1, keepdims=True) > 0.5
        )
        allowed = jnp.logical_and(same, is_valid) | jnp.logical_not(last)
        tables[w] = jnp.where(allowed, wide, NEGATIVE)


def one_window(flat_f, flat_c, chosen, gain, proj_weight, weights, bias, eye, head_masks):
    x = nn(chosen, flat_f)
    cot = nn(chosen, flat_c).astype(BF16)
    yield
    mean = jnp.mean(x, axis=1, keepdims=True)
    centered = x - mean
    variance = jnp.mean(centered * centered, axis=1, keepdims=True)
    inverse = lax.rsqrt(variance + EPSILON)
    hat = centered * inverse
    normed = (hat * gain).astype(BF16)
    yield
    queries = nn(normed, weights[0]).astype(BF16)
    keys = nn(normed, weights[1]).astype(BF16)
    values = nn(normed, weights[2]).astype(BF16)
    keys_t = keys.T
    values_t = values.T
    grad_att = nt(cot, proj_weight).astype(BF16)
    yield
    q_blocks = head_blocks(queries, head_masks)
    g_blocks = head_blocks(grad_att, head_masks)
    scores = nt(keys, q_blocks) * (SCALE * LOG2E) + bias
    yield
    exponent = jnp.exp2(scores - jnp.max(scores, axis=0, keepdims=True))
    soft = exponent * (1.0 / jnp.sum(exponent, axis=0, keepdims=True))
    yield
    soft_bf = soft.astype(BF16)
    grad_soft = nt(values, g_blocks)
    yield
    delta = jnp.sum(soft * grad_soft, axis=0, keepdims=True)
    grad_scores = soft * (grad_soft - delta)
    yield
    grad_bf = grad_scores.astype(BF16)
    grad_values = nn(soft_bf, g_blocks).astype(BF16)
    grad_keys = (nn(grad_bf, q_blocks) * SCALE).astype(BF16)
    yield
    attended_t = own_heads(nn(values_t, soft_bf)).astype(BF16)
    grad_queries_t = (own_heads(nn(keys_t, grad_bf)) * SCALE).astype(BF16)
    yield
    projected_t = nn(weights[5], attended_t).astype(BF16)
    projected = projected_t.T
    grad_queries = grad_queries_t.T
    yield
    grad_normed = (
        nt(grad_queries, weights[0]) + nt(grad_keys, weights[1]) + nt(grad_values, weights[2])
    )
    yield
    grad_hat = grad_normed * gain
    grad_x = inverse * (
        grad_hat
        - jnp.mean(grad_hat, axis=1, keepdims=True)
        - hat * jnp.mean(grad_hat * hat, axis=1, keepdims=True)
    )
    return projected, grad_x.astype(BF16), grad_scores


def together(windows):
    results = [None] * len(windows)
    left = dict(enumerate(windows))
    while left:
        for n in list(left):
            try:
                next(left[n])
            except StopIteration as end:
                results[n] = end.value
                del left[n]
    return results


def run_windows(todo, r, tables, group):
    features = r["fields"].shape[-1]
    lane_head = lax.broadcasted_iota(jnp.int32, (1, features), 1) // HEAD_DIM
    head_masks = [(lane_head == h).astype(F32).astype(BF16) for h in range(HEADS)]
    eye = r["eye"][...]
    windows = []
    for pair in range(group):
        levels = slice(WZ * pair, WZ * (pair + 1))
        halos = {k: unpack(r[k][pair]) for k in ("east", "south", "far") if k in r}
        for b, w in todo:
            flats = []
            for n, ref in enumerate((r["fields"], r["cot"])):
                columns = slice(SLON, SLON + WLON) if w == 0 else slice(SLON + WLON, COLS)
                parts = [ref[levels, columns].reshape(-1, features)]
                if w == 1:
                    parts.append(halos["east"][n])
                if b == 1:
                    parts.append(halos["south"][n])
                    if w == 1:
                        parts.append(halos["far"][n])
                flats.append(jnp.concatenate(parts, axis=0))
            windows.append(
                one_window(
                    *flats,
                    r["pick%d" % w][...],
                    r["gain"][...],
                    r["proj"][...],
                    r["weights"],
                    tables(w),
                    eye,
                    head_masks,
                )
            )
    done = together(windows)
    total = done[0][2]
    for _, _, scores in done[1:]:
        total = total + scores
    each = len(todo)
    return [[d[:2] for d in done[each * p : each * (p + 1)]] for p in range(group)], total


def first_kernel(names, group, *refs):
    r = dict(zip(names, refs))

    @pl.when(pl.program_id(0) == 0)
    def start():
        prepare_weights(r["qkv"], r["proj"], r["eye"][...], r["weights"])
        r["table"][...] = wide_bias(0, r["bias"], r["bias_pick"])
        r["sum"][...] = jnp.zeros_like(r["sum"])

    pairs, total = run_windows([(0, 1)], r, lambda w: r["table"][...], group)
    for pair, done in enumerate(pairs):
        r["win_p"][pair], r["win_g"][pair] = done[0]
    r["sum"][...] += total


def south_kernel(names, group, *refs):
    r = dict(zip(names, refs))

    @pl.when(pl.program_id(0) == 0)
    def start():
        wide = wide_bias(1, r["bias"], r["bias_pick"])
        masked_tables(wide, r["at"], r["valid"], r["tables"])
        r["sum"][...] = jnp.zeros_like(r["sum"])

    pairs, total = run_windows([(1, 0), (1, 1)], r, lambda w: r["tables"][w], group)
    r["sum"][...] += total
    for pair, done in enumerate(pairs):
        placed = []
        for n, (first, out) in enumerate(
            ((r["first_p"], r["win_p"]), (r["first_g"], r["win_g"]))
        ):
            both = jnp.concatenate([done[0][n], done[1][n]], axis=0)
            out[pair] = both
            placed.append(nn(r["place"][...], jnp.concatenate([first[pair], both], axis=0)))
        r["west"][pair] = pack(*(p[:STRIP] for p in placed))
        r["north"][pair] = pack(*(p[STRIP : 2 * STRIP] for p in placed))
        r["corner"][pair] = pack(*(p[2 * STRIP :] for p in placed))


def last_kernel(names, group, *refs):
    r = dict(zip(names, refs))
    step = pl.program_id(0)

    @pl.when(step == 0)
    def start():
        r["sum"][...] = r["sum0"][...]

    pairs, total = run_windows([(0, 0)], r, lambda w: r["table"][...], group)
    r["sum"][...] += total
    for pair, done in enumerate(pairs):
        r["win_p"][pair], r["win_g"][pair] = done[0]

    @pl.when(step == pl.num_programs(0) - 1)
    def finish():
        out = r["bias_out"]
        for b, ref in enumerate((r["sum"], r["sum1"])):
            wide = nt(ref[...].astype(BF16), r["bias_pick"][...])
            top, low = wide[:80], wide[80:]
            for k in range(out.shape[0]):
                left = top[:, k * ROWS : (k + 1) * ROWS]
                right = low[:, k * ROWS : (k + 1) * ROWS]
                right = jnp.concatenate([right, jnp.zeros((160 - WIN, ROWS), F32)], axis=0)
                block = jnp.concatenate([left, right], axis=1).astype(BF16)
                out[k, 80 * b : 80 * (b + 1)] = block


def land_kernel(
    fields_ref,
    cot_ref,
    last_p_ref,
    last_g_ref,
    first_p_ref,
    first_g_ref,
    south_p_ref,
    south_g_ref,
    west_ref,
    north_ref,
    far_ref,
    place_ref,
    out_m_ref,
    out_g_ref,
):
    kinds = (
        (fields_ref, (last_p_ref, first_p_ref, south_p_ref), out_m_ref),
        (cot_ref, (last_g_ref, first_g_ref, south_g_ref), out_g_ref),
    )
    for pair in range(west_ref.shape[0]):
        strips = [unpack(ref[pair]) for ref in (west_ref, north_ref, far_ref)]
        levels = slice(WZ * pair, WZ * (pair + 1))
        for n, (base, wins, out) in enumerate(kinds):
            own = base[levels]
            pieces = [ref[pair] for ref in wins] + [strip[n] for strip in strips]
            part = nn(place_ref[...], jnp.concatenate(pieces, axis=0))
            out[levels] = (own.astype(F32) + part.reshape(own.shape)).astype(BF16)


def bias_kernel(bias_ref, out_ref):
    count = out_ref.shape[0]
    total = bias_ref[0].astype(F32)
    for k in range(1, bias_ref.shape[0]):
        total = total + bias_ref[k].astype(F32)
    for b in range(2):
        turned = total[80 * b : 80 * (b + 1)].T
        whole = jnp.concatenate([turned[:ROWS], turned[ROWS:, : WIN - 80]], axis=1)
        out_ref[:, b, :] = whole[:count]


def by_pair(array, size=1):
    return pl.BlockSpec((size,) + array.shape[1:], lambda g: (g,) + (0,) * (array.ndim - 1))


def whole(array):
    return pl.BlockSpec(array.shape, lambda g: (0,) * array.ndim)


def shape_of(*dims, kind=BF16):
    return jax.ShapeDtypeStruct(dims, kind)


def call(body, name, steps, inputs, outputs, scratch=(), flops=10**9, aliases=()):
    in_specs = [spec for _, spec in inputs]
    bytes_moved = sum(a.size * a.dtype.itemsize for a, _ in inputs) + sum(
        int(np.prod(a.shape)) * a.dtype.itemsize for a, _ in outputs
    )
    return pl.pallas_call(
        body,
        name=name,
        grid=(steps,),
        out_shape=tuple(a for a, _ in outputs),
        in_specs=in_specs,
        out_specs=tuple(spec for _, spec in outputs),
        scratch_shapes=list(scratch),
        input_output_aliases=dict(aliases),
        compiler_params=pltpu.CompilerParams(vmem_limit_bytes=64 * 1024 * 1024),
        cost_estimate=pl.CostEstimate(
            flops=flops, bytes_accessed=bytes_moved, transcendentals=0
        ),
    )(*(a for a, _ in inputs))


def paired(array, size=1):
    return (array, by_pair(array, size))


def entire(array):
    return (array, whole(array))


def in_smem(array):
    return (array, pl.BlockSpec(memory_space=pltpu.SMEM))


def attend(body, name, steps, inputs, outputs, scratch=()):
    scratch = dict(scratch)
    names = list(inputs) + list(outputs) + list(scratch)
    group = inputs["fields"][1].block_shape[0] // WZ
    results = call(
        functools.partial(body, names, group),
        name,
        steps,
        list(inputs.values()),
        list(outputs.values()),
        list(scratch.values()),
        10**10,
    )
    return dict(zip(outputs, results))


def shift(block, lat_step, lon_step):
    lats, lons = lax.axis_size("lat"), lax.axis_size("lon")
    route = [
        (((a + lat_step) % lats) * lons + (o + lon_step) % lons, a * lons + o)
        for a in range(lats)
        for o in range(lons)
    ]
    return lax.ppermute(block, ("lat", "lon"), route)


def local(
    fields, cotangent, norm_gain, qkv_weight, proj_weight, bias_table, window_types, valid_mask
):
    fields = fields.transpose(0, 2, 1, 3)
    cotangent = cotangent.transpose(0, 2, 1, 3)
    levels, lon_cells, lat_cells, features = fields.shape
    lat_at = lax.axis_index("lat")
    lon_at = lax.axis_index("lon")
    parts = lax.axis_size("lon")
    per = WIN // parts
    pairs = levels // WZ
    at = jnp.stack([lat_at, lon_at, lax.axis_size("lat")]).astype(jnp.int32)
    strip = shape_of(pairs, 3 * STRIP, MAIN)
    corner = shape_of(pairs, 3 * CORNER, MAIN)

    table = bias_table.transpose(1, 2, 0, 3).reshape(HEADS * per, -1, WIN)
    (mine,) = call(
        choose_kernel,
        "choose",
        1,
        [
            in_smem(at),
            in_smem(window_types),
            entire(table),
            entire(jnp.asarray(np.eye(WIN), BF16)),
        ],
        [entire(shape_of(parts, WIN, 2 * ROWS))],
    )
    east, south, far = call(
        pack_kernel,
        "pack",
        1,
        [entire(fields), entire(cotangent), entire(jnp.asarray(send_picks(), BF16))],
        [entire(strip), entire(strip), entire(corner)],
    )
    east = shift(east, 0, 1)
    bias = lax.all_to_all(mine, "lon", 0, 0, tiled=True)
    south, far, bias = lax.optimization_barrier((south, far, bias))
    south = shift(south, 1, 0)
    far = shift(far, 1, 1)

    gain = norm_gain.reshape(1, -1)
    windows = {(b, w): window(b, w) for b in range(2) for w in range(2)}
    steps = 1
    group = pairs // steps

    def constant(rows):
        return entire(jnp.asarray(rows, BF16))

    def split(array):
        return paired(array, group)

    def strip_of(count):
        return split(shape_of(pairs, 3 * count, MAIN))

    def tokens_of(count):
        return split(shape_of(pairs, count, features))

    def picked(b, w):
        return constant(pick(windows[b, w], sources_of(b, w)))

    wide_sum = entire(shape_of(WIN, LANES, kind=F32))
    common = {
        "fields": paired(fields, WZ * group),
        "cot": paired(cotangent, WZ * group),
        "gain": entire(gain),
        "proj": entire(proj_weight),
        "eye": constant(np.eye(features)),
    }
    bias_pick = constant(bias_picks(parts))
    first = attend(
        first_kernel,
        "attend_first",
        steps,
        common
        | {
            "east": split(east),
            "qkv": entire(qkv_weight),
            "bias": entire(bias),
            "bias_pick": bias_pick,
            "pick1": picked(0, 1),
        },
        {
            "win_p": tokens_of(WIN),
            "win_g": tokens_of(WIN),
            "weights": entire(shape_of(6, features, features)),
            "table": wide_sum,
            "sum": wide_sum,
        },
    )
    order = [(windows[0, 1] + windows[1, 0] + windows[1, 1], 3 * WIN)]
    place = [
        padded(pick(EAST, order), STRIP),
        padded(pick(SOUTH, order), STRIP),
        padded(pick(FAR, order), CORNER),
    ]
    below = attend(
        south_kernel,
        "attend_south",
        steps,
        common
        | {
            "at": in_smem(at),
            "east": split(east),
            "south": split(south),
            "far": split(far),
            "first_p": split(first["win_p"]),
            "first_g": split(first["win_g"]),
            "weights": entire(first["weights"]),
            "bias": entire(bias),
            "valid": entire(valid_mask),
            "bias_pick": bias_pick,
            "pick0": picked(1, 0),
            "pick1": picked(1, 1),
            "place": constant(np.concatenate(place)),
        },
        {
            "win_p": tokens_of(2 * WIN),
            "win_g": tokens_of(2 * WIN),
            "west": strip_of(STRIP),
            "north": strip_of(STRIP),
            "corner": strip_of(CORNER),
            "sum": wide_sum,
        },
        {"tables": pltpu.VMEM((2, WIN, LANES), F32)},
    )
    north = shift(below["north"], -1, 0)
    far_back = shift(below["corner"], -1, -1)
    west = shift(below["west"], 0, -1)
    last = attend(
        last_kernel,
        "attend_last",
        steps,
        common
        | {
            "weights": entire(first["weights"]),
            "table": entire(first["table"]),
            "sum0": entire(first["sum"]),
            "sum1": entire(below["sum"]),
            "bias_pick": bias_pick,
            "pick0": picked(0, 0),
        },
        {
            "win_p": tokens_of(WIN),
            "win_g": tokens_of(WIN),
            "bias_out": entire(shape_of(parts, 160, 2 * ROWS)),
        },
        {"sum": pltpu.VMEM((WIN, LANES), F32)},
    )
    bias_sums = lax.all_to_all(last["bias_out"], "lon", 0, 0, tiled=True)

    out_bias = shape_of(HEADS * per, 2, WIN, kind=F32)
    steps, group = 2, pairs // 2
    block = paired(shape_of(*fields.shape), WZ * group)
    mixed, grad = call(
        land_kernel,
        "land",
        steps,
        [
            paired(fields, WZ * group),
            paired(cotangent, WZ * group),
            split(last["win_p"]),
            split(last["win_g"]),
            split(first["win_p"]),
            split(first["win_g"]),
            split(below["win_p"]),
            split(below["win_g"]),
            split(west),
            split(north),
            split(far_back),
            constant(land_picks()),
        ],
        [block, block],
        flops=10**11,
    )
    (grad_bias,) = call(bias_kernel, "bias_sum", 1, [entire(bias_sums)], [entire(out_bias)])
    grad_bias = grad_bias.reshape(HEADS, per, 2, WIN).transpose(2, 0, 1, 3)
    return mixed.transpose(0, 2, 1, 3), grad.transpose(0, 2, 1, 3), grad_bias


def solution(mesh):
    in_specs = (
        P(None, "lat", "lon", None),
        P(None, "lat", "lon", None),
        P(),
        P(),
        P(),
        P(None, None, "lon", None),
        P(),
        P(),
    )
    out_specs = (
        P(None, "lat", "lon", None),
        P(None, "lat", "lon", None),
        P("lat", None, "lon", None),
    )
    return jax.shard_map(local, mesh=mesh, in_specs=in_specs, out_specs=out_specs, check_vma=False)
```

```python
import functools

import jax
import jax.numpy as jnp
import numpy as np
from jax import lax
from jax.experimental import pallas as pl
from jax.experimental.pallas import tpu as pltpu
from jax.sharding import PartitionSpec as P

HEADS = 6
WZ = 2
WLAT = 12
WLON = 6
WIN = 144
SLAT = 6
SLON = 3
HEAD_DIM = 32
MAIN = 128
REST = WIN - MAIN
LANES = 896
ROWS = 64

NEGATIVE = -1e30
EPSILON = 1e-05
LOG2E = 1.4426950408889634
SCALE = float(HEAD_DIM) ** (-0.5)

F32 = jnp.float32
BF16 = jnp.bfloat16


def nn(a, b):
    return lax.dot_general(a, b, (((1,), (0,)), ((), ())), preferred_element_type=F32)


def nt(a, b):
    return lax.dot_general(a, b, (((1,), (1,)), ((), ())), preferred_element_type=F32)


def tn(a, b):
    return lax.dot_general(a, b, (((0,), (0,)), ((), ())), preferred_element_type=F32)


def lane_of(head, query):
    return np.where(query < MAIN, head * MAIN + query, HEADS * MAIN + head * REST + query - MAIN)


COLS = 2 * WLON
LATS = 2 * WLAT
PAIR = WZ * COLS * LATS
STRIP = 112
CORNER = 36


def tokens(columns, rows):
    return [(z, c, r) for z in range(WZ) for c in columns for r in rows]


def window(b, w):
    return [
        (z, SLON + WLON * w + c, SLAT + WLAT * b + r)
        for z in range(WZ)
        for r in range(WLAT)
        for c in range(WLON)
    ]


def pick(wanted, sources):
    where, at = {}, 0
    for source, length in sources:
        for n, token in enumerate(source):
            where.setdefault(token, at + n)
        at += length
    out = np.zeros((len(wanted), at), np.float32)
    for n, token in enumerate(wanted):
        if token in where:
            out[n, where[token]] = 1
    return out


def padded(rows, length):
    return np.pad(rows, ((0, length - rows.shape[0]), (0, 0)))


OWN_WEST = tokens(range(SLON, SLON + WLON), range(LATS))
OWN_EAST = tokens(range(SLON + WLON, COLS), range(LATS))
EAST_COLUMNS = range(COLS, COLS + SLON)
EAST = tokens(EAST_COLUMNS, range(SLAT, LATS))
SOUTH = tokens(range(SLON, COLS), range(LATS, LATS + SLAT))
FAR = tokens(EAST_COLUMNS, range(LATS, LATS + SLAT))


def sources_of(b, w):
    if w == 0:
        parts = [(OWN_WEST, len(OWN_WEST))]
    else:
        parts = [(OWN_EAST, len(OWN_EAST)), (EAST, STRIP)]
    if b == 1:
        parts.append((SOUTH, STRIP))
        if w == 1:
            parts.append((FAR, CORNER))
    return parts


def send_picks():
    own = [(tokens(range(COLS), range(LATS)), PAIR)]
    west = pick(tokens(range(SLON), range(SLAT, LATS)), own)
    north = pick(tokens(range(SLON, COLS), range(SLAT)), own)
    corner = pick(tokens(range(SLON), range(SLAT)), own)
    return np.concatenate([padded(west, STRIP), padded(north, STRIP), padded(corner, CORNER + 4)])


def land_picks():
    sources = [
        (window(0, 0), WIN),
        (window(0, 1), WIN),
        (window(1, 0) + window(1, 1), 2 * WIN),
        (tokens(range(SLON), range(SLAT, LATS)), STRIP),
        (tokens(range(SLON, COLS), range(SLAT)), STRIP),
        (tokens(range(SLON), range(SLAT)), CORNER),
    ]
    return pick(tokens(range(COLS), range(LATS)), sources)


def bias_picks(parts):
    per = WIN // parts
    pick = np.zeros((parts, ROWS, LANES), np.float32)
    for k in range(parts):
        for h in range(HEADS):
            for r in range(per):
                pick[k, h * per + r, lane_of(h, k * per + r)] = 1
    return pick.reshape(parts * ROWS, LANES)


def head_blocks(tokens, head_masks):
    pieces = [tokens[:MAIN] * head_masks[h] for h in range(HEADS)]
    pieces += [tokens[MAIN:] * head_masks[h] for h in range(HEADS)]
    pieces.append(jnp.zeros((LANES - HEADS * WIN, tokens.shape[1]), tokens.dtype))
    return jnp.concatenate(pieces, axis=0)


def per_head(left, right):
    main = []
    for h in range(0, HEADS, 2):
        both = nn(
            left[h * HEAD_DIM : (h + 2) * HEAD_DIM], right[:, h * MAIN : (h + 2) * MAIN]
        )
        main += [both[:HEAD_DIM, :MAIN], both[HEAD_DIM:, MAIN:]]
    wide = nn(left, right[:, HEADS * MAIN :])
    rest = [
        wide[h * HEAD_DIM : (h + 1) * HEAD_DIM, h * REST : (h + 1) * REST] for h in range(HEADS)
    ]
    return jnp.concatenate(
        [jnp.concatenate(main, axis=0), jnp.concatenate(rest, axis=0)], axis=1
    )


def pack(rows_a, rows_b):
    return jnp.concatenate(
        [
            rows_a[:, :MAIN],
            rows_b[:, :MAIN],
            jnp.concatenate([rows_a[:, MAIN:], rows_b[:, MAIN:]], axis=1),
        ],
        axis=0,
    ).astype(BF16)


def unpack(packed):
    count = packed.shape[0] // 3
    half = packed.shape[1] // 2
    last = packed[2 * count :]
    return (
        jnp.concatenate([packed[:count], last[:, :half]], axis=1),
        jnp.concatenate([packed[count : 2 * count], last[:, half:]], axis=1),
    )


def choose_kernel(at_ref, types_ref, table_ref, eye_ref, mine_ref):
    table = table_ref[...].astype(F32)
    kind = lax.broadcasted_iota(jnp.int32, (1, table.shape[1], 1), 1)
    chosen = []
    for b in range(2):
        one = jnp.sum(jnp.where(kind == types_ref[2 * at_ref[0] + b], table, 0.0), axis=1)
        chosen.append(one.astype(BF16))
        chosen.append(jnp.zeros((ROWS - one.shape[0], WIN), BF16))
    mine = nt(eye_ref[...], jnp.concatenate(chosen, axis=0)).astype(BF16)
    mine_ref[...] = jnp.broadcast_to(mine[None], mine_ref.shape)


def pack_kernel(fields_ref, cot_ref, pick_ref, east_ref, south_ref, far_ref):
    features = fields_ref.shape[-1]
    for g in range(east_ref.shape[0]):
        rows = [
            nn(pick_ref[...], ref[WZ * g : WZ * (g + 1)].reshape(-1, features))
            for ref in (fields_ref, cot_ref)
        ]
        at = 0
        for ref, count in ((east_ref, STRIP), (south_ref, STRIP), (far_ref, CORNER)):
            ref[g] = pack(*(r[at : at + count] for r in rows))
            at += count


def prepare_weights(qkv_ref, proj_ref, eye, weights):
    features = proj_ref.shape[0]
    for n in range(3):
        weights[n] = qkv_ref[:, n * features : (n + 1) * features]
    weights[3] = nt(eye, weights[1]).astype(BF16)
    weights[4] = nt(eye, weights[2]).astype(BF16)
    weights[5] = nt(eye, proj_ref[...]).astype(BF16)


def wide_bias(b, bias_ref, bias_pick_ref):
    table = jnp.concatenate(
        [bias_ref[k, :, b * ROWS : (b + 1) * ROWS] for k in range(bias_ref.shape[0])], axis=1
    )
    return nn(table, bias_pick_ref[...]) * LOG2E


def masked_tables(wide, at_ref, valid_ref, tables):
    key = lax.broadcasted_iota(jnp.int32, (WIN, 1), 0)
    lane = lax.broadcasted_iota(jnp.int32, (1, LANES), 1)
    query = jnp.where(lane < HEADS * MAIN, lane % MAIN, MAIN + (lane - HEADS * MAIN) % REST)
    key_row = (key // WLON) % WLAT
    query_row = (query // WLON) % WLAT
    last = at_ref[0] == at_ref[2] - 1
    same = (key_row < SLAT) == (query_row < SLAT)
    lat_rows, lon_columns = valid_ref.shape
    valid_rows = jnp.concatenate(
        [valid_ref[lat_rows - SLAT :, :], valid_ref[:SLAT, :]], axis=0
    ).astype(F32)
    row_pick = (key_row == lax.broadcasted_iota(jnp.int32, (WIN, WLAT), 1)).astype(F32)
    key_valid = nn(row_pick, valid_rows)
    column = lax.broadcasted_iota(jnp.int32, (WIN, lon_columns), 1)
    for w in range(2):
        wanted = at_ref[1] * COLS + SLON + WLON * w + key % WLON
        wanted = jnp.where(wanted >= lon_columns, wanted - lon_columns, wanted)
        is_valid = (
            jnp.sum(jnp.where(column == wanted, key_valid, 0.0), axis=1, keepdims=True) > 0.5
        )
        allowed = jnp.logical_and(same, is_valid) | jnp.logical_not(last)
        tables[w] = jnp.where(allowed, wide, NEGATIVE)


def one_window(flat_f, flat_c, chosen, gain, proj_weight, weights, bias, eye, head_masks):
    x = nn(chosen, flat_f)
    cot = nn(chosen, flat_c).astype(BF16)
    yield
    mean = jnp.mean(x, axis=1, keepdims=True)
    centered = x - mean
    variance = jnp.mean(centered * centered, axis=1, keepdims=True)
    inverse = lax.rsqrt(variance + EPSILON)
    hat = centered * inverse
    normed = (hat * gain).astype(BF16)
    yield
    queries = nn(normed, weights[0]).astype(BF16)
    keys = nn(normed, weights[1]).astype(BF16)
    values = nn(normed, weights[2]).astype(BF16)
    keys_t = keys.T
    values_t = values.T
    grad_att = nt(cot, proj_weight).astype(BF16)
    yield
    q_blocks = head_blocks(queries, head_masks)
    g_blocks = head_blocks(grad_att, head_masks)
    scores = nt(keys, q_blocks) * (SCALE * LOG2E) + bias
    yield
    exponent = jnp.exp2(scores - jnp.max(scores, axis=0, keepdims=True))
    soft = exponent * (1.0 / jnp.sum(exponent, axis=0, keepdims=True))
    yield
    soft_bf = soft.astype(BF16)
    grad_soft = nt(values, g_blocks)
    yield
    delta = jnp.sum(soft * grad_soft, axis=0, keepdims=True)
    grad_scores = soft * (grad_soft - delta)
    yield
    grad_bf = grad_scores.astype(BF16)
    grad_values = nn(soft_bf, g_blocks).astype(BF16)
    grad_keys = (nn(grad_bf, q_blocks) * SCALE).astype(BF16)
    yield
    attended_t = per_head(values_t, soft_bf).astype(BF16)
    grad_queries_t = (per_head(keys_t, grad_bf) * SCALE).astype(BF16)
    yield
    projected_t = nn(weights[5], attended_t).astype(BF16)
    projected = projected_t.T
    grad_queries = grad_queries_t.T
    yield
    grad_normed = (
        nt(grad_queries, weights[0]) + nt(grad_keys, weights[1]) + nt(grad_values, weights[2])
    )
    yield
    grad_hat = grad_normed * gain
    grad_x = inverse * (
        grad_hat
        - jnp.mean(grad_hat, axis=1, keepdims=True)
        - hat * jnp.mean(grad_hat * hat, axis=1, keepdims=True)
    )
    return projected, grad_x.astype(BF16), grad_scores


def together(windows):
    results = [None] * len(windows)
    left = dict(enumerate(windows))
    while left:
        for n in list(left):
            try:
                next(left[n])
            except StopIteration as end:
                results[n] = end.value
                del left[n]
    return results


def run_windows(todo, r, tables):
    features = r["fields"].shape[-1]
    lane_head = lax.broadcasted_iota(jnp.int32, (1, features), 1) // HEAD_DIM
    head_masks = [(lane_head == h).astype(F32).astype(BF16) for h in range(HEADS)]
    eye = r["eye"][...]
    halos = {}
    windows = []
    for pair, b, w in todo:
        levels = slice(WZ * pair, WZ * (pair + 1))
        for k in ("east", "south", "far"):
            if k in r and (k, pair) not in halos:
                halos[k, pair] = unpack(r[k][pair])
        flats = []
        for n, ref in enumerate((r["fields"], r["cot"])):
            columns = slice(SLON, SLON + WLON) if w == 0 else slice(SLON + WLON, COLS)
            parts = [ref[levels, columns].reshape(-1, features)]
            if w == 1:
                parts.append(halos["east", pair][n])
            if b == 1:
                parts.append(halos["south", pair][n])
                if w == 1:
                    parts.append(halos["far", pair][n])
            flats.append(jnp.concatenate(parts, axis=0))
        windows.append(
            one_window(
                *flats,
                r["pick%d" % w][...],
                r["gain"][...],
                r["proj"][...],
                r["weights"],
                tables(w),
                eye,
                head_masks,
            )
        )
    done = together(windows)
    total = done[0][2]
    for _, _, scores in done[1:]:
        total = total + scores
    return [d[:2] for d in done], total


def first_kernel(names, group, *refs):
    r = dict(zip(names, refs))

    @pl.when(pl.program_id(0) == 0)
    def start():
        prepare_weights(r["qkv"], r["proj"], r["eye"][...], r["weights"])
        r["table"][...] = wide_bias(0, r["bias"], r["bias_pick"])
        r["sum"][...] = jnp.zeros_like(r["sum"])

    inner = r["in_p"].shape[0]
    todo = [(pair, 0, 1) for pair in range(group)] + [(pair, 0, 0) for pair in range(inner)]
    done, total = run_windows(todo, r, lambda w: r["table"][...])
    for pair in range(group):
        r["win_p"][pair], r["win_g"][pair] = done[pair]
    for pair in range(inner):
        r["in_p"][pair], r["in_g"][pair] = done[group + pair]
    r["sum"][...] += total


def south_kernel(names, group, *refs):
    r = dict(zip(names, refs))

    @pl.when(pl.program_id(0) == 0)
    def start():
        wide = wide_bias(1, r["bias"], r["bias_pick"])
        masked_tables(wide, r["at"], r["valid"], r["tables"])
        r["sum"][...] = jnp.zeros_like(r["sum"])

    todo = [(pair, 1, w) for pair in range(group) for w in range(2)]
    results, total = run_windows(todo, r, lambda w: r["tables"][w])
    r["sum"][...] += total
    for pair in range(group):
        done = results[2 * pair : 2 * pair + 2]
        placed = []
        for n, (first, out) in enumerate(
            ((r["first_p"], r["win_p"]), (r["first_g"], r["win_g"]))
        ):
            both = jnp.concatenate([done[0][n], done[1][n]], axis=0)
            out[pair] = both
            placed.append(nn(r["place"][...], jnp.concatenate([first[pair], both], axis=0)))
        r["west"][pair] = pack(*(p[:STRIP] for p in placed))
        r["north"][pair] = pack(*(p[STRIP : 2 * STRIP] for p in placed))
        r["corner"][pair] = pack(*(p[2 * STRIP : 2 * STRIP + CORNER] for p in placed))


def last_kernel(names, group, *refs):
    r = dict(zip(names, refs))
    step = pl.program_id(0)

    @pl.when(step == 0)
    def start():
        r["sum"][...] = r["sum0"][...]

    todo = [(pair, 0, 0) for pair in range(group)]
    done, total = run_windows(todo, r, lambda w: r["table"][...])
    r["sum"][...] += total
    for pair in range(group):
        r["win_p"][pair], r["win_g"][pair] = done[pair]

    @pl.when(step == pl.num_programs(0) - 1)
    def finish():
        wide = [nt(r[n][...].astype(BF16), r["bias_pick"][...]) for n in ("sum", "sum1")]
        for k in range(r["bias_out"].shape[0]):
            blocks = [part[:, k * ROWS : (k + 1) * ROWS] for part in wide]
            r["bias_out"][k] = jnp.concatenate(blocks, axis=1).astype(BF16)


def land_kernel(
    fields_ref,
    cot_ref,
    in_p_ref,
    in_g_ref,
    last_p_ref,
    last_g_ref,
    first_p_ref,
    first_g_ref,
    south_p_ref,
    south_g_ref,
    west_ref,
    north_ref,
    far_ref,
    place_ref,
    out_m_ref,
    out_g_ref,
):
    kinds = (
        (fields_ref, (in_p_ref, last_p_ref), (first_p_ref, south_p_ref), out_m_ref),
        (cot_ref, (in_g_ref, last_g_ref), (first_g_ref, south_g_ref), out_g_ref),
    )
    early = pl.program_id(0) == 0
    for pair in range(west_ref.shape[0]):
        strips = [unpack(ref[pair]) for ref in (west_ref, north_ref, far_ref)]
        levels = slice(WZ * pair, WZ * (pair + 1))
        for n, (base, inner, wins, out) in enumerate(kinds):
            own = base[levels]
            pieces = [jnp.where(early, inner[0][pair], inner[1][pair])]
            pieces += [ref[pair] for ref in wins] + [strip[n] for strip in strips]
            part = nn(place_ref[...], jnp.concatenate(pieces, axis=0))
            out[levels] = (own.astype(F32) + part.reshape(own.shape)).astype(BF16)


def bias_kernel(bias_ref, out_ref):
    count = out_ref.shape[0]
    total = bias_ref[0].astype(F32)
    for k in range(1, bias_ref.shape[0]):
        total = total + bias_ref[k].astype(F32)
    turned = total.T
    for b in range(2):
        out_ref[:, b, :] = turned[b * ROWS : b * ROWS + count]


def by_pair(array, size=1):
    return pl.BlockSpec((size,) + array.shape[1:], lambda g: (g,) + (0,) * (array.ndim - 1))


def whole(array):
    return pl.BlockSpec(array.shape, lambda g: (0,) * array.ndim)


def shape_of(*dims, kind=BF16):
    return jax.ShapeDtypeStruct(dims, kind)


def call(body, name, steps, inputs, outputs, scratch=(), flops=10**9, aliases=()):
    in_specs = [spec for _, spec in inputs]
    bytes_moved = sum(a.size * a.dtype.itemsize for a, _ in inputs) + sum(
        int(np.prod(a.shape)) * a.dtype.itemsize for a, _ in outputs
    )
    return pl.pallas_call(
        body,
        name=name,
        grid=(steps,),
        out_shape=tuple(a for a, _ in outputs),
        in_specs=in_specs,
        out_specs=tuple(spec for _, spec in outputs),
        scratch_shapes=list(scratch),
        input_output_aliases=dict(aliases),
        compiler_params=pltpu.CompilerParams(vmem_limit_bytes=64 * 1024 * 1024),
        cost_estimate=pl.CostEstimate(
            flops=flops, bytes_accessed=bytes_moved, transcendentals=0
        ),
    )(*(a for a, _ in inputs))


def paired(array, size=1):
    return (array, by_pair(array, size))


def entire(array):
    return (array, whole(array))


def in_smem(array):
    return (array, pl.BlockSpec(memory_space=pltpu.SMEM))


def attend(body, name, steps, inputs, outputs, scratch=()):
    scratch = dict(scratch)
    names = list(inputs) + list(outputs) + list(scratch)
    group = inputs["fields"][1].block_shape[0] // WZ
    results = call(
        functools.partial(body, names, group),
        name,
        steps,
        list(inputs.values()),
        list(outputs.values()),
        list(scratch.values()),
        10**10,
    )
    return dict(zip(outputs, results))


def shift(block, lat_step, lon_step):
    lats, lons = lax.axis_size("lat"), lax.axis_size("lon")
    route = [
        (((a + lat_step) % lats) * lons + (o + lon_step) % lons, a * lons + o)
        for a in range(lats)
        for o in range(lons)
    ]
    return lax.ppermute(block, ("lat", "lon"), route)


def local(
    fields, cotangent, norm_gain, qkv_weight, proj_weight, bias_table, window_types, valid_mask
):
    fields = fields.transpose(0, 2, 1, 3)
    cotangent = cotangent.transpose(0, 2, 1, 3)
    levels, lon_cells, lat_cells, features = fields.shape
    lat_at = lax.axis_index("lat")
    lon_at = lax.axis_index("lon")
    parts = lax.axis_size("lon")
    per = WIN // parts
    pairs = levels // WZ
    at = jnp.stack([lat_at, lon_at, lax.axis_size("lat")]).astype(jnp.int32)
    strip = shape_of(pairs, 3 * STRIP, MAIN)
    corner = shape_of(pairs, 3 * CORNER, MAIN)

    table = bias_table.transpose(1, 2, 0, 3).reshape(HEADS * per, -1, WIN)
    (mine,) = call(
        choose_kernel,
        "choose",
        1,
        [
            in_smem(at),
            in_smem(window_types),
            entire(table),
            entire(jnp.asarray(np.eye(WIN), BF16)),
        ],
        [entire(shape_of(parts, WIN, 2 * ROWS))],
    )
    east, south, far = call(
        pack_kernel,
        "pack",
        1,
        [entire(fields), entire(cotangent), entire(jnp.asarray(send_picks(), BF16))],
        [entire(strip), entire(strip), entire(corner)],
    )
    east = shift(east, 0, 1)
    bias = lax.all_to_all(mine, "lon", 0, 0, tiled=True)
    south, far, bias = lax.optimization_barrier((south, far, bias))
    south = shift(south, 1, 0)
    far = shift(far, 1, 1)

    gain = norm_gain.reshape(1, -1)
    windows = {(b, w): window(b, w) for b in range(2) for w in range(2)}
    steps = 1
    group = pairs // steps

    def constant(rows):
        return entire(jnp.asarray(rows, BF16))

    def split(array):
        return paired(array, group)

    def strip_of(count):
        return split(shape_of(pairs, 3 * count, MAIN))

    def tokens_of(count):
        return split(shape_of(pairs, count, features))

    def picked(b, w):
        return constant(pick(windows[b, w], sources_of(b, w)))

    wide_sum = entire(shape_of(WIN, LANES, kind=F32))
    common = {
        "fields": paired(fields, WZ * group),
        "cot": paired(cotangent, WZ * group),
        "gain": entire(gain),
        "proj": entire(proj_weight),
        "eye": constant(np.eye(features)),
    }
    bias_pick = constant(bias_picks(parts))
    half = entire(shape_of(pairs // 2, WIN, features))
    upper = pl.BlockSpec((levels // 2,) + fields.shape[1:], lambda g: (1, 0, 0, 0))
    first = attend(
        first_kernel,
        "attend_first",
        steps,
        common
        | {
            "east": split(east),
            "qkv": entire(qkv_weight),
            "bias": entire(bias),
            "bias_pick": bias_pick,
            "pick0": picked(0, 0),
            "pick1": picked(0, 1),
        },
        {
            "win_p": tokens_of(WIN),
            "win_g": tokens_of(WIN),
            "in_p": half,
            "in_g": half,
            "weights": entire(shape_of(6, features, features)),
            "table": wide_sum,
            "sum": wide_sum,
        },
    )
    order = [(windows[0, 1] + windows[1, 0] + windows[1, 1], 3 * WIN)]
    place = [
        padded(pick(EAST, order), STRIP),
        padded(pick(SOUTH, order), STRIP),
        padded(pick(FAR, order), CORNER + 4),
    ]
    below = attend(
        south_kernel,
        "attend_south",
        steps,
        common
        | {
            "at": in_smem(at),
            "east": split(east),
            "south": split(south),
            "far": split(far),
            "first_p": split(first["win_p"]),
            "first_g": split(first["win_g"]),
            "weights": entire(first["weights"]),
            "bias": entire(bias),
            "valid": entire(valid_mask),
            "bias_pick": bias_pick,
            "pick0": picked(1, 0),
            "pick1": picked(1, 1),
            "place": constant(np.concatenate(place)),
        },
        {
            "win_p": tokens_of(2 * WIN),
            "win_g": tokens_of(2 * WIN),
            "west": strip_of(STRIP),
            "north": strip_of(STRIP),
            "corner": strip_of(CORNER),
            "sum": wide_sum,
        },
        {"tables": pltpu.VMEM((2, WIN, LANES), F32)},
    )
    north = shift(below["north"], -1, 0)
    far_back = shift(below["corner"], -1, -1)
    west = shift(below["west"], 0, -1)
    last = attend(
        last_kernel,
        "attend_last",
        steps,
        common
        | {
            "fields": (fields, upper),
            "cot": (cotangent, upper),
            "weights": entire(first["weights"]),
            "table": entire(first["table"]),
            "sum0": entire(first["sum"]),
            "sum1": entire(below["sum"]),
            "bias_pick": bias_pick,
            "pick0": picked(0, 0),
        },
        {
            "win_p": half,
            "win_g": half,
            "bias_out": entire(shape_of(parts, WIN, 2 * ROWS)),
        },
        {"sum": pltpu.VMEM((WIN, LANES), F32)},
    )
    bias_sums = lax.all_to_all(last["bias_out"], "lon", 0, 0, tiled=True)

    out_bias = shape_of(HEADS * per, 2, WIN, kind=F32)
    steps, group = 2, pairs // 2
    block = paired(shape_of(*fields.shape), WZ * group)
    mixed, grad = call(
        land_kernel,
        "land",
        steps,
        [
            paired(fields, WZ * group),
            paired(cotangent, WZ * group),
            entire(first["in_p"]),
            entire(first["in_g"]),
            entire(last["win_p"]),
            entire(last["win_g"]),
            split(first["win_p"]),
            split(first["win_g"]),
            split(below["win_p"]),
            split(below["win_g"]),
            split(west),
            split(north),
            split(far_back),
            constant(land_picks()),
        ],
        [block, block],
        flops=10**11,
    )
    (grad_bias,) = call(bias_kernel, "bias_sum", 1, [entire(bias_sums)], [entire(out_bias)])
    grad_bias = grad_bias.reshape(HEADS, per, 2, WIN).transpose(2, 0, 1, 3)
    return mixed.transpose(0, 2, 1, 3), grad.transpose(0, 2, 1, 3), grad_bias


def solution(mesh):
    in_specs = (
        P(None, "lat", "lon", None),
        P(None, "lat", "lon", None),
        P(),
        P(),
        P(),
        P(None, None, "lon", None),
        P(),
        P(),
    )
    out_specs = (
        P(None, "lat", "lon", None),
        P(None, "lat", "lon", None),
        P("lat", None, "lon", None),
    )
    return jax.shard_map(local, mesh=mesh, in_specs=in_specs, out_specs=out_specs, check_vma=False)
```

```python
import functools

import jax
import jax.numpy as jnp
import numpy as np
from jax import lax
from jax.experimental import pallas as pl
from jax.experimental.pallas import tpu as pltpu
from jax.sharding import PartitionSpec as P

HEADS = 6
WZ = 2
WLAT = 12
WLON = 6
WIN = 144
SLAT = 6
SLON = 3
HEAD_DIM = 32
MAIN = 128
REST = WIN - MAIN
LANES = 896
ROWS = 64

NEGATIVE = -1e30
EPSILON = 1e-05
LOG2E = 1.4426950408889634
SCALE = float(HEAD_DIM) ** (-0.5)

F32 = jnp.float32
BF16 = jnp.bfloat16


def nn(a, b):
    return lax.dot_general(a, b, (((1,), (0,)), ((), ())), preferred_element_type=F32)


def nt(a, b):
    return lax.dot_general(a, b, (((1,), (1,)), ((), ())), preferred_element_type=F32)


def tn(a, b):
    return lax.dot_general(a, b, (((0,), (0,)), ((), ())), preferred_element_type=F32)


def lane_of(head, query):
    return np.where(query < MAIN, head * MAIN + query, HEADS * MAIN + head * REST + query - MAIN)


COLS = 2 * WLON
LATS = 2 * WLAT
PAIR = WZ * COLS * LATS
STRIP = 112
CORNER = 36
WEST = 72


def tokens(columns, rows):
    return [(z, c, r) for z in range(WZ) for c in columns for r in rows]


def window(b, w):
    return [
        (z, SLON + WLON * w + c, SLAT + WLAT * b + r)
        for z in range(WZ)
        for r in range(WLAT)
        for c in range(WLON)
    ]


def pick(wanted, sources):
    where, at = {}, 0
    for source, length in sources:
        for n, token in enumerate(source):
            where.setdefault(token, at + n)
        at += length
    out = np.zeros((len(wanted), at), np.float32)
    for n, token in enumerate(wanted):
        if token in where:
            out[n, where[token]] = 1
    return out


def padded(rows, length):
    return np.pad(rows, ((0, length - rows.shape[0]), (0, 0)))


OWN_WEST = tokens(range(SLON, SLON + WLON), range(LATS))
OWN_EAST = tokens(range(SLON + WLON, COLS), range(LATS))
EAST_COLUMNS = range(COLS, COLS + SLON)
EAST = tokens(EAST_COLUMNS, range(SLAT, LATS))
SOUTH = tokens(range(SLON, COLS), range(LATS, LATS + SLAT))
FAR = tokens(EAST_COLUMNS, range(LATS, LATS + SLAT))


def sources_of(b, w):
    if w == 0:
        parts = [(OWN_WEST, len(OWN_WEST))]
    else:
        parts = [(OWN_EAST, len(OWN_EAST)), (EAST, STRIP)]
    if b == 1:
        parts.append((SOUTH, STRIP))
        if w == 1:
            parts.append((FAR, CORNER))
    return parts


def send_picks():
    own = [(tokens(range(COLS), range(LATS)), PAIR)]
    west = pick(tokens(range(SLON), range(SLAT, LATS)), own)
    north = pick(tokens(range(SLON, COLS), range(SLAT)), own)
    corner = pick(tokens(range(SLON), range(SLAT)), own)
    return np.concatenate([padded(west, STRIP), padded(north, STRIP), padded(corner, CORNER + 4)])


def land_picks():
    sources = [
        (window(0, 0), WIN),
        (window(0, 1), WIN),
        (window(1, 0) + window(1, 1), 2 * WIN),
        (tokens(range(SLON, COLS), range(SLAT)), STRIP),
        (tokens(range(SLON), range(SLAT, SLAT + WLAT)), WEST),
        (tokens(range(SLON), range(SLAT + WLAT, LATS)), CORNER),
        (tokens(range(SLON), range(SLAT)), CORNER),
    ]
    return pick(tokens(range(COLS), range(LATS)), sources)


def bias_picks(parts):
    per = WIN // parts
    pick = np.zeros((parts, ROWS, LANES), np.float32)
    for k in range(parts):
        for h in range(HEADS):
            for r in range(per):
                pick[k, h * per + r, lane_of(h, k * per + r)] = 1
    return pick.reshape(parts * ROWS, LANES)


def head_blocks(tokens, head_masks):
    pieces = [tokens[:MAIN] * head_masks[h] for h in range(HEADS)]
    pieces += [tokens[MAIN:] * head_masks[h] for h in range(HEADS)]
    pieces.append(jnp.zeros((LANES - HEADS * WIN, tokens.shape[1]), tokens.dtype))
    return jnp.concatenate(pieces, axis=0)


def per_head(left, right):
    main = []
    for h in range(0, HEADS, 2):
        both = nn(
            left[h * HEAD_DIM : (h + 2) * HEAD_DIM], right[:, h * MAIN : (h + 2) * MAIN]
        )
        main += [both[:HEAD_DIM, :MAIN], both[HEAD_DIM:, MAIN:]]
    wide = nn(left, right[:, HEADS * MAIN :])
    rest = [
        wide[h * HEAD_DIM : (h + 1) * HEAD_DIM, h * REST : (h + 1) * REST] for h in range(HEADS)
    ]
    return jnp.concatenate(
        [jnp.concatenate(main, axis=0), jnp.concatenate(rest, axis=0)], axis=1
    )


def pack(rows_a, rows_b):
    return jnp.concatenate(
        [
            rows_a[:, :MAIN],
            rows_b[:, :MAIN],
            jnp.concatenate([rows_a[:, MAIN:], rows_b[:, MAIN:]], axis=1),
        ],
        axis=0,
    ).astype(BF16)


def unpack(packed):
    count = packed.shape[0] // 3
    half = packed.shape[1] // 2
    last = packed[2 * count :]
    return (
        jnp.concatenate([packed[:count], last[:, :half]], axis=1),
        jnp.concatenate([packed[count : 2 * count], last[:, half:]], axis=1),
    )


def choose_kernel(types_ref, table_ref, eye_ref, mine_ref):
    table = table_ref[...].astype(F32)
    kind = lax.broadcasted_iota(jnp.int32, (1, table.shape[1], 1), 1)
    chosen = []
    for b in range(2):
        one = jnp.sum(jnp.where(kind == types_ref[2 * lax.axis_index("lat") + b], table, 0.0), axis=1)
        chosen.append(one.astype(BF16))
        chosen.append(jnp.zeros((ROWS - one.shape[0], WIN), BF16))
    mine = nt(eye_ref[...], jnp.concatenate(chosen, axis=0)).astype(BF16)
    mine_ref[...] = jnp.broadcast_to(mine[None], mine_ref.shape)


def pack_kernel(fields_ref, cot_ref, pick_ref, east_ref, south_ref, far_ref):
    features = fields_ref.shape[-1]
    for g in range(east_ref.shape[0]):
        rows = [
            nn(pick_ref[...], ref[WZ * g : WZ * (g + 1)].reshape(-1, features))
            for ref in (fields_ref, cot_ref)
        ]
        at = 0
        for ref, count in ((east_ref, STRIP), (south_ref, STRIP), (far_ref, CORNER)):
            ref[g] = pack(*(r[at : at + count] for r in rows))
            at += count


def prepare_weights(qkv_ref, proj_ref, eye, weights):
    features = proj_ref.shape[0]
    for n in range(3):
        weights[n] = qkv_ref[:, n * features : (n + 1) * features]
    weights[3] = nt(eye, weights[1]).astype(BF16)
    weights[4] = nt(eye, weights[2]).astype(BF16)
    weights[5] = nt(eye, proj_ref[...]).astype(BF16)


def wide_bias(b, bias_ref, bias_pick_ref):
    table = jnp.concatenate(
        [bias_ref[k, :, b * ROWS : (b + 1) * ROWS] for k in range(bias_ref.shape[0])], axis=1
    )
    return nn(table, bias_pick_ref[...]) * LOG2E


def masked_tables(wide, valid_ref, tables):
    key = lax.broadcasted_iota(jnp.int32, (WIN, 1), 0)
    lane = lax.broadcasted_iota(jnp.int32, (1, LANES), 1)
    query = jnp.where(lane < HEADS * MAIN, lane % MAIN, MAIN + (lane - HEADS * MAIN) % REST)
    key_row = (key // WLON) % WLAT
    query_row = (query // WLON) % WLAT
    last = lax.axis_index("lat") == lax.axis_size("lat") - 1
    same = (key_row < SLAT) == (query_row < SLAT)
    lat_rows, lon_columns = valid_ref.shape
    valid_rows = jnp.concatenate(
        [valid_ref[lat_rows - SLAT :, :], valid_ref[:SLAT, :]], axis=0
    ).astype(F32)
    row_pick = (key_row == lax.broadcasted_iota(jnp.int32, (WIN, WLAT), 1)).astype(F32)
    key_valid = nn(row_pick, valid_rows)
    column = lax.broadcasted_iota(jnp.int32, (WIN, lon_columns), 1)
    for w in range(2):
        wanted = lax.axis_index("lon") * COLS + SLON + WLON * w + key % WLON
        wanted = jnp.where(wanted >= lon_columns, wanted - lon_columns, wanted)
        is_valid = (
            jnp.sum(jnp.where(column == wanted, key_valid, 0.0), axis=1, keepdims=True) > 0.5
        )
        allowed = jnp.logical_and(same, is_valid) | jnp.logical_not(last)
        tables[w] = jnp.where(allowed, wide, NEGATIVE)


def one_window(flat_f, flat_c, chosen, gain, proj_weight, weights, bias, eye, head_masks):
    x = nn(chosen, flat_f)
    cot = nn(chosen, flat_c).astype(BF16)
    yield
    mean = jnp.mean(x, axis=1, keepdims=True)
    centered = x - mean
    variance = jnp.mean(centered * centered, axis=1, keepdims=True)
    inverse = lax.rsqrt(variance + EPSILON)
    hat = centered * inverse
    normed = (hat * gain).astype(BF16)
    yield
    queries = nn(normed, weights[0]).astype(BF16)
    keys = nn(normed, weights[1]).astype(BF16)
    values = nn(normed, weights[2]).astype(BF16)
    keys_t = keys.T
    values_t = values.T
    grad_att = nt(cot, proj_weight).astype(BF16)
    yield
    q_blocks = head_blocks(queries, head_masks)
    g_blocks = head_blocks(grad_att, head_masks)
    scores = nt(keys, q_blocks) * (SCALE * LOG2E) + bias
    yield
    exponent = jnp.exp2(scores - jnp.max(scores, axis=0, keepdims=True))
    soft = exponent * (1.0 / jnp.sum(exponent, axis=0, keepdims=True))
    yield
    soft_bf = soft.astype(BF16)
    grad_soft = nt(values, g_blocks)
    yield
    delta = jnp.sum(soft * grad_soft, axis=0, keepdims=True)
    grad_scores = soft * (grad_soft - delta)
    yield
    grad_bf = grad_scores.astype(BF16)
    grad_values = nn(soft_bf, g_blocks).astype(BF16)
    grad_keys = (nn(grad_bf, q_blocks) * SCALE).astype(BF16)
    yield
    attended_t = per_head(values_t, soft_bf).astype(BF16)
    grad_queries_t = (per_head(keys_t, grad_bf) * SCALE).astype(BF16)
    yield
    projected_t = nn(weights[5], attended_t).astype(BF16)
    projected = projected_t.T
    grad_queries = grad_queries_t.T
    yield
    grad_normed = (
        nt(grad_queries, weights[0]) + nt(grad_keys, weights[1]) + nt(grad_values, weights[2])
    )
    yield
    grad_hat = grad_normed * gain
    grad_x = inverse * (
        grad_hat
        - jnp.mean(grad_hat, axis=1, keepdims=True)
        - hat * jnp.mean(grad_hat * hat, axis=1, keepdims=True)
    )
    return projected, grad_x.astype(BF16), grad_scores


def together(windows):
    results = [None] * len(windows)
    left = dict(enumerate(windows))
    while left:
        for n in list(left):
            try:
                next(left[n])
            except StopIteration as end:
                results[n] = end.value
                del left[n]
    return results


def run_windows(todo, r, tables):
    features = r["fields"].shape[-1]
    lane_head = lax.broadcasted_iota(jnp.int32, (1, features), 1) // HEAD_DIM
    head_masks = [(lane_head == h).astype(F32).astype(BF16) for h in range(HEADS)]
    eye = r["eye"][...]
    halos = {}
    windows = []
    for pair, b, w in todo:
        levels = slice(WZ * pair, WZ * (pair + 1))
        for k in ("east", "south", "far"):
            if k in r and (k, pair) not in halos:
                halos[k, pair] = unpack(r[k][pair])
        flats = []
        for n, ref in enumerate((r["fields"], r["cot"])):
            columns = slice(SLON, SLON + WLON) if w == 0 else slice(SLON + WLON, COLS)
            parts = [ref[levels, columns].reshape(-1, features)]
            if w == 1:
                parts.append(halos["east", pair][n])
            if b == 1:
                parts.append(halos["south", pair][n])
                if w == 1:
                    parts.append(halos["far", pair][n])
            flats.append(jnp.concatenate(parts, axis=0))
        windows.append(
            one_window(
                *flats,
                r["pick%d" % w][...],
                r["gain"][...],
                r["proj"][...],
                r["weights"],
                tables(w),
                eye,
                head_masks,
            )
        )
    done = together(windows)
    total = done[0][2]
    for _, _, scores in done[1:]:
        total = total + scores
    return [d[:2] for d in done], total


def first_kernel(names, group, *refs):
    r = dict(zip(names, refs))

    @pl.when(pl.program_id(0) == 0)
    def start():
        prepare_weights(r["qkv"], r["proj"], r["eye"][...], r["weights"])
        r["table"][...] = wide_bias(0, r["bias"], r["bias_pick"])
        r["sum"][...] = jnp.zeros_like(r["sum"])

    inner = r["in_p"].shape[0]
    todo = [(pair, 0, 1) for pair in range(group)] + [(pair, 0, 0) for pair in range(inner)]
    done, total = run_windows(todo, r, lambda w: r["table"][...])
    for pair in range(group):
        r["win_p"][pair], r["win_g"][pair] = done[pair]
        r["west"][pair] = pack(*(nn(r["place"][...], part) for part in done[pair]))
    for pair in range(inner):
        r["in_p"][pair], r["in_g"][pair] = done[group + pair]
    r["sum"][...] += total


def south_kernel(names, group, *refs):
    r = dict(zip(names, refs))

    @pl.when(pl.program_id(0) == 0)
    def start():
        wide = wide_bias(1, r["bias"], r["bias_pick"])
        masked_tables(wide, r["valid"], r["tables"])
        r["sum"][...] = jnp.zeros_like(r["sum"])

    todo = [(pair, 1, w) for pair in range(group) for w in range(2)]
    results, total = run_windows(todo, r, lambda w: r["tables"][w])
    r["sum"][...] += total
    for pair in range(group):
        done = results[2 * pair : 2 * pair + 2]
        placed = []
        for n, out in enumerate((r["win_p"], r["win_g"])):
            both = jnp.concatenate([done[0][n], done[1][n]], axis=0)
            out[pair] = both
            placed.append(nn(r["place"][...], both))
        r["north"][pair] = pack(*(p[:STRIP] for p in placed))
        r["west"][pair] = pack(*(p[STRIP : STRIP + CORNER] for p in placed))
        at = STRIP + CORNER + 4
        r["corner"][pair] = pack(*(p[at : at + CORNER] for p in placed))


def last_kernel(names, group, *refs):
    r = dict(zip(names, refs))
    late = [
        pltpu.make_async_copy(r[n], r[n + "_here"], r["arrived"].at[k])
        for k, n in enumerate(("bias_pick", "sum0", "sum1"))
    ]
    for copy in late:
        copy.start()
    todo = [(pair, 0, 0) for pair in range(group)]
    done, total = run_windows(todo, r, lambda w: r["table"][...])
    for pair in range(group):
        r["win_p"][pair], r["win_g"][pair] = done[pair]
    for pair in range(r["west"].shape[0]):
        r["west_p"][pair], r["west_g"][pair] = unpack(r["west"][pair])
    for copy in late:
        copy.wait()
    sums = (r["sum0_here"][...] + total, r["sum1_here"][...])
    wide = [nt(part.astype(BF16), r["bias_pick_here"][...]) for part in sums]
    for k in range(r["bias_out"].shape[0]):
        blocks = [part[:, k * ROWS : (k + 1) * ROWS] for part in wide]
        r["bias_out"][k] = jnp.concatenate(blocks, axis=1).astype(BF16)


def land_kernel(
    fields_ref,
    cot_ref,
    in_p_ref,
    in_g_ref,
    last_p_ref,
    last_g_ref,
    first_p_ref,
    first_g_ref,
    south_p_ref,
    south_g_ref,
    west_p_ref,
    west_g_ref,
    west_ref,
    north_ref,
    far_ref,
    place_ref,
    out_m_ref,
    out_g_ref,
):
    kinds = (
        (fields_ref, (in_p_ref, last_p_ref), (first_p_ref, south_p_ref), west_p_ref, out_m_ref),
        (cot_ref, (in_g_ref, last_g_ref), (first_g_ref, south_g_ref), west_g_ref, out_g_ref),
    )
    early = pl.program_id(0) == 0
    for pair in range(west_ref.shape[0]):
        strips = [unpack(ref[pair]) for ref in (north_ref, west_ref, far_ref)]
        levels = slice(WZ * pair, WZ * (pair + 1))
        for n, (base, inner, wins, edge, out) in enumerate(kinds):
            own = base[levels]
            pieces = [jnp.where(early, inner[0][pair], inner[1][pair])]
            pieces += [ref[pair] for ref in wins]
            pieces += [strips[0][n], edge[pair], strips[1][n], strips[2][n]]
            part = nn(place_ref[...], jnp.concatenate(pieces, axis=0))
            out[levels] = (own.astype(F32) + part.reshape(own.shape)).astype(BF16)


def bias_kernel(bias_ref, out_ref):
    count = out_ref.shape[0]
    total = bias_ref[0].astype(F32)
    for k in range(1, bias_ref.shape[0]):
        total = total + bias_ref[k].astype(F32)
    turned = total.T
    for b in range(2):
        out_ref[:, b, :] = turned[b * ROWS : b * ROWS + count]


def by_pair(array, size=1):
    return pl.BlockSpec((size,) + array.shape[1:], lambda g: (g,) + (0,) * (array.ndim - 1))


def whole(array):
    return pl.BlockSpec(array.shape, lambda g: (0,) * array.ndim)


def shape_of(*dims, kind=BF16):
    return jax.ShapeDtypeStruct(dims, kind)


def call(body, name, steps, inputs, outputs, scratch=(), flops=10**9, aliases=()):
    in_specs = [spec for _, spec in inputs]
    bytes_moved = sum(a.size * a.dtype.itemsize for a, _ in inputs) + sum(
        int(np.prod(a.shape)) * a.dtype.itemsize for a, _ in outputs
    )
    return pl.pallas_call(
        body,
        name=name,
        grid=(steps,),
        out_shape=tuple(a for a, _ in outputs),
        in_specs=in_specs,
        out_specs=tuple(spec for _, spec in outputs),
        scratch_shapes=list(scratch),
        input_output_aliases=dict(aliases),
        compiler_params=pltpu.CompilerParams(vmem_limit_bytes=64 * 1024 * 1024),
        cost_estimate=pl.CostEstimate(
            flops=flops, bytes_accessed=bytes_moved, transcendentals=0
        ),
    )(*(a for a, _ in inputs))


def paired(array, size=1):
    return (array, by_pair(array, size))


def entire(array):
    return (array, whole(array))


def in_place(array):
    return (array, pl.BlockSpec(memory_space=pl.ANY))


def in_smem(array):
    return (array, pl.BlockSpec(memory_space=pltpu.SMEM))


def attend(body, name, steps, inputs, outputs, scratch=()):
    scratch = dict(scratch)
    names = list(inputs) + list(outputs) + list(scratch)
    group = inputs["fields"][1].block_shape[0] // WZ
    results = call(
        functools.partial(body, names, group),
        name,
        steps,
        list(inputs.values()),
        list(outputs.values()),
        list(scratch.values()),
        10**10,
    )
    return dict(zip(outputs, results))


def shift(block, lat_step, lon_step):
    lats, lons = lax.axis_size("lat"), lax.axis_size("lon")
    route = [
        (((a + lat_step) % lats) * lons + (o + lon_step) % lons, a * lons + o)
        for a in range(lats)
        for o in range(lons)
    ]
    return lax.ppermute(block, ("lat", "lon"), route)


def local(
    fields, cotangent, norm_gain, qkv_weight, proj_weight, bias_table, window_types, valid_mask
):
    fields = fields.transpose(0, 2, 1, 3)
    cotangent = cotangent.transpose(0, 2, 1, 3)
    levels, lon_cells, lat_cells, features = fields.shape
    parts = lax.axis_size("lon")
    per = WIN // parts
    pairs = levels // WZ
    strip = shape_of(pairs, 3 * STRIP, MAIN)
    corner = shape_of(pairs, 3 * CORNER, MAIN)

    table = bias_table.transpose(1, 2, 0, 3).reshape(HEADS * per, -1, WIN)
    (mine,) = call(
        choose_kernel,
        "choose",
        1,
        [
            in_smem(window_types),
            entire(table),
            entire(jnp.asarray(np.eye(WIN), BF16)),
        ],
        [entire(shape_of(parts, WIN, 2 * ROWS))],
    )
    east, south, far = call(
        pack_kernel,
        "pack",
        1,
        [entire(fields), entire(cotangent), entire(jnp.asarray(send_picks(), BF16))],
        [entire(strip), entire(strip), entire(corner)],
    )
    east = shift(east, 0, 1)
    bias = lax.all_to_all(mine, "lon", 0, 0, tiled=True)
    south, far, bias = lax.optimization_barrier((south, far, bias))
    south = shift(south, 1, 0)
    far = shift(far, 1, 1)

    gain = norm_gain.reshape(1, -1)
    windows = {(b, w): window(b, w) for b in range(2) for w in range(2)}
    steps = 1
    group = pairs // steps

    def constant(rows):
        return entire(jnp.asarray(rows, BF16))

    def split(array):
        return paired(array, group)

    def strip_of(count):
        return split(shape_of(pairs, 3 * count, MAIN))

    def tokens_of(count):
        return split(shape_of(pairs, count, features))

    def picked(b, w):
        return constant(pick(windows[b, w], sources_of(b, w)))

    wide_sum = entire(shape_of(WIN, LANES, kind=F32))
    common = {
        "fields": paired(fields, WZ * group),
        "cot": paired(cotangent, WZ * group),
        "gain": entire(gain),
        "proj": entire(proj_weight),
        "eye": constant(np.eye(features)),
    }
    bias_pick = constant(bias_picks(parts))
    half = entire(shape_of(pairs // 2, WIN, features))
    upper = pl.BlockSpec((levels // 2,) + fields.shape[1:], lambda g: (1, 0, 0, 0))
    first = attend(
        first_kernel,
        "attend_first",
        steps,
        common
        | {
            "east": split(east),
            "qkv": entire(qkv_weight),
            "bias": entire(bias),
            "bias_pick": bias_pick,
            "pick0": picked(0, 0),
            "pick1": picked(0, 1),
            "place": constant(
                pick(
                    tokens(EAST_COLUMNS, range(SLAT, SLAT + WLAT)), [(windows[0, 1], WIN)]
                )
            ),
        },
        {
            "west": strip_of(WEST),
            "win_p": tokens_of(WIN),
            "win_g": tokens_of(WIN),
            "in_p": half,
            "in_g": half,
            "weights": entire(shape_of(6, features, features)),
            "table": wide_sum,
            "sum": wide_sum,
        },
    )
    west0 = shift(first["west"], 0, -1)
    order = [(windows[1, 0] + windows[1, 1], 2 * WIN)]
    place = [
        padded(pick(SOUTH, order), STRIP),
        padded(pick(tokens(EAST_COLUMNS, range(SLAT + WLAT, LATS)), order), CORNER + 4),
        padded(pick(FAR, order), CORNER + 4),
    ]
    below = attend(
        south_kernel,
        "attend_south",
        steps,
        common
        | {
            "east": split(east),
            "south": split(south),
            "far": split(far),
            "weights": entire(first["weights"]),
            "bias": entire(bias),
            "valid": entire(valid_mask),
            "bias_pick": bias_pick,
            "pick0": picked(1, 0),
            "pick1": picked(1, 1),
            "place": constant(np.concatenate(place)),
        },
        {
            "win_p": tokens_of(2 * WIN),
            "win_g": tokens_of(2 * WIN),
            "west": strip_of(CORNER),
            "north": strip_of(STRIP),
            "corner": strip_of(CORNER),
            "sum": wide_sum,
        },
        {"tables": pltpu.VMEM((2, WIN, LANES), F32)},
    )
    north = shift(below["north"], -1, 0)
    far_back = shift(below["corner"], -1, -1)
    west = shift(below["west"], 0, -1)
    last = attend(
        last_kernel,
        "attend_last",
        steps,
        common
        | {
            "fields": (fields, upper),
            "cot": (cotangent, upper),
            "weights": entire(first["weights"]),
            "table": entire(first["table"]),
            "west": entire(west0),
            "sum0": in_place(first["sum"]),
            "sum1": in_place(below["sum"]),
            "bias_pick": in_place(bias_pick[0]),
            "pick0": picked(0, 0),
        },
        {
            "win_p": half,
            "win_g": half,
            "west_p": tokens_of(WEST),
            "west_g": tokens_of(WEST),
            "bias_out": entire(shape_of(parts, WIN, 2 * ROWS)),
        },
        {
            "sum0_here": pltpu.VMEM((WIN, LANES), F32),
            "sum1_here": pltpu.VMEM((WIN, LANES), F32),
            "bias_pick_here": pltpu.VMEM((parts * ROWS, LANES), BF16),
            "arrived": pltpu.SemaphoreType.DMA((3,)),
        },
    )
    bias_sums = lax.all_to_all(last["bias_out"], "lon", 0, 0, tiled=True)

    out_bias = shape_of(HEADS * per, 2, WIN, kind=F32)
    steps, group = 2, pairs // 2
    block = paired(shape_of(*fields.shape), WZ * group)
    mixed, grad = call(
        land_kernel,
        "land",
        steps,
        [
            paired(fields, WZ * group),
            paired(cotangent, WZ * group),
            entire(first["in_p"]),
            entire(first["in_g"]),
            entire(last["win_p"]),
            entire(last["win_g"]),
            split(first["win_p"]),
            split(first["win_g"]),
            split(below["win_p"]),
            split(below["win_g"]),
            split(last["west_p"]),
            split(last["west_g"]),
            split(west),
            split(north),
            split(far_back),
            constant(land_picks()),
        ],
        [block, block],
        flops=10**11,
    )
    (grad_bias,) = call(bias_kernel, "bias_sum", 1, [entire(bias_sums)], [entire(out_bias)])
    grad_bias = grad_bias.reshape(HEADS, per, 2, WIN).transpose(2, 0, 1, 3)
    return mixed.transpose(0, 2, 1, 3), grad.transpose(0, 2, 1, 3), grad_bias


def solution(mesh):
    in_specs = (
        P(None, "lat", "lon", None),
        P(None, "lat", "lon", None),
        P(),
        P(),
        P(),
        P(None, None, "lon", None),
        P(),
        P(),
    )
    out_specs = (
        P(None, "lat", "lon", None),
        P(None, "lat", "lon", None),
        P("lat", None, "lon", None),
    )
    return jax.shard_map(local, mesh=mesh, in_specs=in_specs, out_specs=out_specs, check_vma=False)
```

```python
import functools

import jax
import jax.numpy as jnp
import numpy as np
from jax import lax
from jax.experimental import pallas as pl
from jax.experimental.pallas import tpu as pltpu
from jax.sharding import PartitionSpec as P

HEADS = 6
WZ = 2
WLAT = 12
WLON = 6
WIN = 144
SLAT = 6
SLON = 3
HEAD_DIM = 32
MAIN = 128
REST = WIN - MAIN
LANES = 896
ROWS = 64

NEGATIVE = -1e30
EPSILON = 1e-05
LOG2E = 1.4426950408889634
SCALE = float(HEAD_DIM) ** (-0.5)

F32 = jnp.float32
BF16 = jnp.bfloat16


def nn(a, b):
    return lax.dot_general(a, b, (((1,), (0,)), ((), ())), preferred_element_type=F32)


def nt(a, b):
    return lax.dot_general(a, b, (((1,), (1,)), ((), ())), preferred_element_type=F32)


def tn(a, b):
    return lax.dot_general(a, b, (((0,), (0,)), ((), ())), preferred_element_type=F32)


def lane_of(head, query):
    return np.where(query < MAIN, head * MAIN + query, HEADS * MAIN + head * REST + query - MAIN)


COLS = 2 * WLON
LATS = 2 * WLAT
PAIR = WZ * COLS * LATS
STRIP = 112
CORNER = 36
WEST = 72


def tokens(columns, rows):
    return [(z, c, r) for z in range(WZ) for c in columns for r in rows]


def window(b, w):
    return [
        (z, SLON + WLON * w + c, SLAT + WLAT * b + r)
        for z in range(WZ)
        for r in range(WLAT)
        for c in range(WLON)
    ]


def pick(wanted, sources):
    where, at = {}, 0
    for source, length in sources:
        for n, token in enumerate(source):
            where.setdefault(token, at + n)
        at += length
    out = np.zeros((len(wanted), at), np.float32)
    for n, token in enumerate(wanted):
        if token in where:
            out[n, where[token]] = 1
    return out


def padded(rows, length):
    return np.pad(rows, ((0, length - rows.shape[0]), (0, 0)))


OWN_WEST = tokens(range(SLON, SLON + WLON), range(LATS))
OWN_EAST = tokens(range(SLON + WLON, COLS), range(LATS))
EAST_COLUMNS = range(COLS, COLS + SLON)
EAST = tokens(EAST_COLUMNS, range(SLAT, LATS))
SOUTH = tokens(range(SLON, COLS), range(LATS, LATS + SLAT))
FAR = tokens(EAST_COLUMNS, range(LATS, LATS + SLAT))


def sources_of(b, w):
    if w == 0:
        parts = [(OWN_WEST, len(OWN_WEST))]
    else:
        parts = [(OWN_EAST, len(OWN_EAST)), (EAST, STRIP)]
    if b == 1:
        parts.append((SOUTH, STRIP))
        if w == 1:
            parts.append((FAR, CORNER))
    return parts


def send_picks():
    own = [(tokens(range(COLS), range(LATS)), PAIR)]
    west = pick(tokens(range(SLON), range(SLAT, LATS)), own)
    north = pick(tokens(range(SLON, COLS), range(SLAT)), own)
    corner = pick(tokens(range(SLON), range(SLAT)), own)
    return np.concatenate([padded(west, STRIP), padded(north, STRIP), padded(corner, CORNER + 4)])


def land_picks():
    sources = [
        (window(0, 0), WIN),
        (window(0, 1), WIN),
        (window(1, 0) + window(1, 1), 2 * WIN),
        (tokens(range(SLON, COLS), range(SLAT)), STRIP),
        (tokens(range(SLON), range(SLAT, SLAT + WLAT)), WEST),
        (tokens(range(SLON), range(SLAT + WLAT, LATS)), CORNER),
        (tokens(range(SLON), range(SLAT)), CORNER),
    ]
    return pick(tokens(range(COLS), range(LATS)), sources)


def bias_picks(parts):
    per = WIN // parts
    pick = np.zeros((parts, ROWS, LANES), np.float32)
    for k in range(parts):
        for h in range(HEADS):
            for r in range(per):
                pick[k, h * per + r, lane_of(h, k * per + r)] = 1
    return pick.reshape(parts * ROWS, LANES)


def head_blocks(tokens, head_masks):
    pieces = [tokens[:MAIN] * head_masks[h] for h in range(HEADS)]
    pieces += [tokens[MAIN:] * head_masks[h] for h in range(HEADS)]
    pieces.append(jnp.zeros((LANES - HEADS * WIN, tokens.shape[1]), tokens.dtype))
    return jnp.concatenate(pieces, axis=0)


def per_head(left, right):
    main = []
    for h in range(0, HEADS, 2):
        both = nn(
            left[h * HEAD_DIM : (h + 2) * HEAD_DIM], right[:, h * MAIN : (h + 2) * MAIN]
        )
        main += [both[:HEAD_DIM, :MAIN], both[HEAD_DIM:, MAIN:]]
    wide = nn(left, right[:, HEADS * MAIN :])
    rest = [
        wide[h * HEAD_DIM : (h + 1) * HEAD_DIM, h * REST : (h + 1) * REST] for h in range(HEADS)
    ]
    return jnp.concatenate(
        [jnp.concatenate(main, axis=0), jnp.concatenate(rest, axis=0)], axis=1
    )


def pack(rows_a, rows_b):
    return jnp.concatenate(
        [
            rows_a[:, :MAIN],
            rows_b[:, :MAIN],
            jnp.concatenate([rows_a[:, MAIN:], rows_b[:, MAIN:]], axis=1),
        ],
        axis=0,
    ).astype(BF16)


def unpack(packed):
    count = packed.shape[0] // 3
    half = packed.shape[1] // 2
    last = packed[2 * count :]
    return (
        jnp.concatenate([packed[:count], last[:, :half]], axis=1),
        jnp.concatenate([packed[count : 2 * count], last[:, half:]], axis=1),
    )


def choose_kernel(types_ref, table_ref, eye_ref, mine_ref):
    table = table_ref[...].astype(F32)
    kind = lax.broadcasted_iota(jnp.int32, (1, table.shape[1], 1), 1)
    chosen = []
    for b in range(2):
        one = jnp.sum(jnp.where(kind == types_ref[2 * lax.axis_index("lat") + b], table, 0.0), axis=1)
        chosen.append(one.astype(BF16))
        chosen.append(jnp.zeros((ROWS - one.shape[0], WIN), BF16))
    mine = nt(eye_ref[...], jnp.concatenate(chosen, axis=0)).astype(BF16)
    mine_ref[...] = jnp.broadcast_to(mine[None], mine_ref.shape)


def pack_kernel(fields_ref, cot_ref, pick_ref, east_ref, south_ref, far_ref):
    features = fields_ref.shape[-1]
    for g in range(east_ref.shape[0]):
        rows = [
            nn(pick_ref[...], ref[WZ * g : WZ * (g + 1)].reshape(-1, features))
            for ref in (fields_ref, cot_ref)
        ]
        at = 0
        for ref, count in ((east_ref, STRIP), (south_ref, STRIP), (far_ref, CORNER)):
            ref[g] = pack(*(r[at : at + count] for r in rows))
            at += count


def prepare_weights(qkv_ref, proj_ref, eye, weights):
    features = proj_ref.shape[0]
    for n in range(3):
        weights[n] = qkv_ref[:, n * features : (n + 1) * features]
    weights[3] = nt(eye, weights[1]).astype(BF16)
    weights[4] = nt(eye, weights[2]).astype(BF16)
    weights[5] = nt(eye, proj_ref[...]).astype(BF16)


def wide_bias(b, bias_ref, bias_pick_ref):
    table = jnp.concatenate(
        [bias_ref[k, :, b * ROWS : (b + 1) * ROWS] for k in range(bias_ref.shape[0])], axis=1
    )
    return nn(table, bias_pick_ref[...]) * LOG2E


def masked_tables(wide, valid_ref, tables):
    key = lax.broadcasted_iota(jnp.int32, (WIN, 1), 0)
    lane = lax.broadcasted_iota(jnp.int32, (1, LANES), 1)
    query = jnp.where(lane < HEADS * MAIN, lane % MAIN, MAIN + (lane - HEADS * MAIN) % REST)
    key_row = (key // WLON) % WLAT
    query_row = (query // WLON) % WLAT
    last = lax.axis_index("lat") == lax.axis_size("lat") - 1
    same = (key_row < SLAT) == (query_row < SLAT)
    lat_rows, lon_columns = valid_ref.shape
    valid_rows = jnp.concatenate(
        [valid_ref[lat_rows - SLAT :, :], valid_ref[:SLAT, :]], axis=0
    ).astype(F32)
    row_pick = (key_row == lax.broadcasted_iota(jnp.int32, (WIN, WLAT), 1)).astype(F32)
    key_valid = nn(row_pick, valid_rows)
    column = lax.broadcasted_iota(jnp.int32, (WIN, lon_columns), 1)
    for w in range(2):
        wanted = lax.axis_index("lon") * COLS + SLON + WLON * w + key % WLON
        wanted = jnp.where(wanted >= lon_columns, wanted - lon_columns, wanted)
        is_valid = (
            jnp.sum(jnp.where(column == wanted, key_valid, 0.0), axis=1, keepdims=True) > 0.5
        )
        allowed = jnp.logical_and(same, is_valid) | jnp.logical_not(last)
        tables[w] = jnp.where(allowed, wide, NEGATIVE)


def one_window(flat_f, flat_c, chosen, gain, proj_weight, weights, bias, eye, head_masks):
    x = nn(chosen, flat_f)
    cot = nn(chosen, flat_c).astype(BF16)
    yield
    mean = jnp.mean(x, axis=1, keepdims=True)
    centered = x - mean
    variance = jnp.mean(centered * centered, axis=1, keepdims=True)
    inverse = lax.rsqrt(variance + EPSILON)
    hat = centered * inverse
    normed = (hat * gain).astype(BF16)
    yield
    queries = nn(normed, weights[0]).astype(BF16)
    keys = nn(normed, weights[1]).astype(BF16)
    values = nn(normed, weights[2]).astype(BF16)
    keys_t = keys.T
    values_t = values.T
    grad_att = nt(cot, proj_weight).astype(BF16)
    yield
    q_blocks = head_blocks(queries, head_masks)
    g_blocks = head_blocks(grad_att, head_masks)
    scores = nt(keys, q_blocks) * (SCALE * LOG2E) + bias
    yield
    exponent = jnp.exp2(scores - jnp.max(scores, axis=0, keepdims=True))
    soft = exponent * (1.0 / jnp.sum(exponent, axis=0, keepdims=True))
    yield
    soft_bf = soft.astype(BF16)
    grad_soft = nt(values, g_blocks)
    yield
    delta = jnp.sum(soft * grad_soft, axis=0, keepdims=True)
    grad_scores = soft * (grad_soft - delta)
    yield
    grad_bf = grad_scores.astype(BF16)
    grad_values = nn(soft_bf, g_blocks).astype(BF16)
    grad_keys = (nn(grad_bf, q_blocks) * SCALE).astype(BF16)
    yield
    attended_t = per_head(values_t, soft_bf).astype(BF16)
    grad_queries_t = (per_head(keys_t, grad_bf) * SCALE).astype(BF16)
    yield
    projected_t = nn(weights[5], attended_t).astype(BF16)
    projected = projected_t.T
    grad_queries = grad_queries_t.T
    yield
    grad_normed = (
        nt(grad_queries, weights[0]) + nt(grad_keys, weights[1]) + nt(grad_values, weights[2])
    )
    yield
    grad_hat = grad_normed * gain
    grad_x = inverse * (
        grad_hat
        - jnp.mean(grad_hat, axis=1, keepdims=True)
        - hat * jnp.mean(grad_hat * hat, axis=1, keepdims=True)
    )
    return projected, grad_x.astype(BF16), grad_scores


def together(windows):
    results = [None] * len(windows)
    left = dict(enumerate(windows))
    while left:
        for n in list(left):
            try:
                next(left[n])
            except StopIteration as end:
                results[n] = end.value
                del left[n]
    return results


def run_windows(todo, r, tables):
    features = r["fields"].shape[-1]
    lane_head = lax.broadcasted_iota(jnp.int32, (1, features), 1) // HEAD_DIM
    head_masks = [(lane_head == h).astype(F32).astype(BF16) for h in range(HEADS)]
    eye = r["eye"][...]
    halos = {}
    windows = []
    for pair, b, w in todo:
        levels = slice(WZ * pair, WZ * (pair + 1))
        for k in ("east", "south", "far"):
            if k in r and (k, pair) not in halos:
                halos[k, pair] = unpack(r[k][pair])
        flats = []
        for n, ref in enumerate((r["fields"], r["cot"])):
            columns = slice(SLON, SLON + WLON) if w == 0 else slice(SLON + WLON, COLS)
            parts = [ref[levels, columns].reshape(-1, features)]
            if w == 1:
                parts.append(halos["east", pair][n])
            if b == 1:
                parts.append(halos["south", pair][n])
                if w == 1:
                    parts.append(halos["far", pair][n])
            flats.append(jnp.concatenate(parts, axis=0))
        windows.append(
            one_window(
                *flats,
                r["pick%d" % w][...],
                r["gain"][...],
                r["proj"][...],
                r["weights"],
                tables(w),
                eye,
                head_masks,
            )
        )
    done = together(windows)
    total = done[0][2]
    for _, _, scores in done[1:]:
        total = total + scores
    return [d[:2] for d in done], total


def first_kernel(names, group, *refs):
    r = dict(zip(names, refs))

    @pl.when(pl.program_id(0) == 0)
    def start():
        prepare_weights(r["qkv"], r["proj"], r["eye"][...], r["weights"])
        r["table"][...] = wide_bias(0, r["bias"], r["bias_pick"])
        r["sum"][...] = jnp.zeros_like(r["sum"])

    inner = r["in_p"].shape[0]
    todo = [(pair, 0, 1) for pair in range(group)] + [(pair, 0, 0) for pair in range(inner)]
    done, total = run_windows(todo, r, lambda w: r["table"][...])
    for pair in range(group):
        r["win_p"][pair], r["win_g"][pair] = done[pair]
        r["west"][pair] = pack(*(nn(r["place"][...], part) for part in done[pair]))
    for pair in range(inner):
        r["in_p"][pair], r["in_g"][pair] = done[group + pair]
    r["sum"][...] += total


def south_kernel(names, group, *refs):
    r = dict(zip(names, refs))

    @pl.when(pl.program_id(0) == 0)
    def start():
        wide = wide_bias(1, r["bias"], r["bias_pick"])
        masked_tables(wide, r["valid"], r["tables"])
        r["sum"][...] = jnp.zeros_like(r["sum"])

    todo = [(pair, 1, w) for pair in range(group) for w in range(2)]
    results, total = run_windows(todo, r, lambda w: r["tables"][w])
    r["sum"][...] += total
    for pair in range(group):
        done = results[2 * pair : 2 * pair + 2]
        placed = []
        for n, out in enumerate((r["win_p"], r["win_g"])):
            both = jnp.concatenate([done[0][n], done[1][n]], axis=0)
            out[pair] = both
            placed.append(nn(r["place"][...], both))
        r["north"][pair] = pack(*(p[:STRIP] for p in placed))
        r["west"][pair] = pack(*(p[STRIP : STRIP + CORNER] for p in placed))
        at = STRIP + CORNER + 4
        r["corner"][pair] = pack(*(p[at : at + CORNER] for p in placed))


def last_kernel(names, group, *refs):
    r = dict(zip(names, refs))
    late = [
        pltpu.make_async_copy(r[n], r[n + "_here"], r["arrived"].at[k])
        for k, n in enumerate(("bias_pick", "sum0", "sum1"))
    ]
    for copy in late:
        copy.start()
    todo = [(pair, 0, 0) for pair in range(group)]
    done, total = run_windows(todo, r, lambda w: r["table"][...])
    for pair in range(group):
        r["win_p"][pair], r["win_g"][pair] = done[pair]
    for pair in range(r["west"].shape[0]):
        r["west_p"][pair], r["west_g"][pair] = unpack(r["west"][pair])
    for copy in late:
        copy.wait()
    sums = (r["sum0_here"][...] + total, r["sum1_here"][...])
    wide = [nt(part.astype(BF16), r["bias_pick_here"][...]) for part in sums]
    for k in range(r["bias_out"].shape[0]):
        blocks = [part[:, k * ROWS : (k + 1) * ROWS] for part in wide]
        r["bias_out"][k] = jnp.concatenate(blocks, axis=1).astype(BF16)


def land_kernel(
    fields_ref,
    cot_ref,
    in_p_ref,
    in_g_ref,
    last_p_ref,
    last_g_ref,
    first_p_ref,
    first_g_ref,
    south_p_ref,
    south_g_ref,
    west_p_ref,
    west_g_ref,
    west_ref,
    north_ref,
    far_ref,
    place_ref,
    out_m_ref,
    out_g_ref,
):
    kinds = (
        (fields_ref, (in_p_ref, last_p_ref), (first_p_ref, south_p_ref), west_p_ref, out_m_ref),
        (cot_ref, (in_g_ref, last_g_ref), (first_g_ref, south_g_ref), west_g_ref, out_g_ref),
    )
    early = pl.program_id(0) == 0
    for pair in range(west_ref.shape[0]):
        strips = [unpack(ref[pair]) for ref in (north_ref, west_ref, far_ref)]
        levels = slice(WZ * pair, WZ * (pair + 1))
        for n, (base, inner, wins, edge, out) in enumerate(kinds):
            own = base[levels]
            pieces = [jnp.where(early, inner[0][pair], inner[1][pair])]
            pieces += [ref[pair] for ref in wins]
            pieces += [strips[0][n], edge[pair], strips[1][n], strips[2][n]]
            part = nn(place_ref[...], jnp.concatenate(pieces, axis=0))
            out[levels] = (own.astype(F32) + part.reshape(own.shape)).astype(BF16)


def bias_kernel(bias_ref, out_ref):
    count = out_ref.shape[0]
    total = bias_ref[0].astype(F32)
    for k in range(1, bias_ref.shape[0]):
        total = total + bias_ref[k].astype(F32)
    turned = total.T
    for b in range(2):
        out_ref[:, b, :] = turned[b * ROWS : b * ROWS + count]


def by_pair(array, size=1):
    return pl.BlockSpec((size,) + array.shape[1:], lambda g: (g,) + (0,) * (array.ndim - 1))


def whole(array):
    return pl.BlockSpec(array.shape, lambda g: (0,) * array.ndim)


def shape_of(*dims, kind=BF16):
    return jax.ShapeDtypeStruct(dims, kind)


def call(body, name, steps, inputs, outputs, scratch=(), flops=10**9, aliases=()):
    in_specs = [spec for _, spec in inputs]
    bytes_moved = sum(a.size * a.dtype.itemsize for a, _ in inputs) + sum(
        int(np.prod(a.shape)) * a.dtype.itemsize for a, _ in outputs
    )
    return pl.pallas_call(
        body,
        name=name,
        grid=(steps,),
        out_shape=tuple(a for a, _ in outputs),
        in_specs=in_specs,
        out_specs=tuple(spec for _, spec in outputs),
        scratch_shapes=list(scratch),
        input_output_aliases=dict(aliases),
        compiler_params=pltpu.CompilerParams(vmem_limit_bytes=64 * 1024 * 1024),
        cost_estimate=pl.CostEstimate(
            flops=flops, bytes_accessed=bytes_moved, transcendentals=0
        ),
    )(*(a for a, _ in inputs))


def paired(array, size=1):
    return (array, by_pair(array, size))


def entire(array):
    return (array, whole(array))


def in_place(array):
    return (array, pl.BlockSpec(memory_space=pl.ANY))


def in_smem(array):
    return (array, pl.BlockSpec(memory_space=pltpu.SMEM))


def attend(body, name, steps, inputs, outputs, scratch=()):
    scratch = dict(scratch)
    names = list(inputs) + list(outputs) + list(scratch)
    group = inputs["fields"][1].block_shape[0] // WZ
    results = call(
        functools.partial(body, names, group),
        name,
        steps,
        list(inputs.values()),
        list(outputs.values()),
        list(scratch.values()),
        10**10,
    )
    return dict(zip(outputs, results))


def shift(block, lat_step, lon_step):
    lats, lons = lax.axis_size("lat"), lax.axis_size("lon")
    route = [
        (((a + lat_step) % lats) * lons + (o + lon_step) % lons, a * lons + o)
        for a in range(lats)
        for o in range(lons)
    ]
    return lax.ppermute(block, ("lat", "lon"), route)


def local(
    fields, cotangent, norm_gain, qkv_weight, proj_weight, bias_table, window_types, valid_mask
):
    fields = fields.transpose(0, 2, 1, 3)
    cotangent = cotangent.transpose(0, 2, 1, 3)
    levels, lon_cells, lat_cells, features = fields.shape
    parts = lax.axis_size("lon")
    per = WIN // parts
    pairs = levels // WZ
    strip = shape_of(pairs, 3 * STRIP, MAIN)
    corner = shape_of(pairs, 3 * CORNER, MAIN)

    table = bias_table.transpose(1, 2, 0, 3).reshape(HEADS * per, -1, WIN)
    (mine,) = call(
        choose_kernel,
        "choose",
        1,
        [
            in_smem(window_types),
            entire(table),
            entire(jnp.asarray(np.eye(WIN), BF16)),
        ],
        [entire(shape_of(parts, WIN, 2 * ROWS))],
    )
    east, south, far = call(
        pack_kernel,
        "pack",
        1,
        [entire(fields), entire(cotangent), entire(jnp.asarray(send_picks(), BF16))],
        [entire(strip), entire(strip), entire(corner)],
    )
    east = shift(east, 0, 1)
    bias = lax.all_to_all(mine, "lon", 0, 0, tiled=True)
    south, bias = lax.optimization_barrier((south, bias))
    south = shift(south, 1, 0)
    far = shift(far, 1, 1)

    gain = norm_gain.reshape(1, -1)
    windows = {(b, w): window(b, w) for b in range(2) for w in range(2)}
    steps = 1
    group = pairs // steps

    def constant(rows):
        return entire(jnp.asarray(rows, BF16))

    def split(array):
        return paired(array, group)

    def strip_of(count):
        return split(shape_of(pairs, 3 * count, MAIN))

    def tokens_of(count):
        return split(shape_of(pairs, count, features))

    def picked(b, w):
        return constant(pick(windows[b, w], sources_of(b, w)))

    wide_sum = entire(shape_of(WIN, LANES, kind=F32))
    common = {
        "fields": paired(fields, WZ * group),
        "cot": paired(cotangent, WZ * group),
        "gain": entire(gain),
        "proj": entire(proj_weight),
        "eye": constant(np.eye(features)),
    }
    bias_pick = constant(bias_picks(parts))
    half = entire(shape_of(pairs // 2, WIN, features))
    upper = pl.BlockSpec((levels // 2,) + fields.shape[1:], lambda g: (1, 0, 0, 0))
    first = attend(
        first_kernel,
        "attend_first",
        steps,
        common
        | {
            "east": split(east),
            "qkv": entire(qkv_weight),
            "bias": entire(bias),
            "bias_pick": bias_pick,
            "pick0": picked(0, 0),
            "pick1": picked(0, 1),
            "place": constant(
                pick(
                    tokens(EAST_COLUMNS, range(SLAT, SLAT + WLAT)), [(windows[0, 1], WIN)]
                )
            ),
        },
        {
            "west": strip_of(WEST),
            "win_p": tokens_of(WIN),
            "win_g": tokens_of(WIN),
            "in_p": half,
            "in_g": half,
            "weights": entire(shape_of(6, features, features)),
            "table": wide_sum,
            "sum": wide_sum,
        },
    )
    west0 = shift(first["west"], 0, -1)
    order = [(windows[1, 0] + windows[1, 1], 2 * WIN)]
    place = [
        padded(pick(SOUTH, order), STRIP),
        padded(pick(tokens(EAST_COLUMNS, range(SLAT + WLAT, LATS)), order), CORNER + 4),
        padded(pick(FAR, order), CORNER + 4),
    ]
    below = attend(
        south_kernel,
        "attend_south",
        steps,
        common
        | {
            "east": split(east),
            "south": split(south),
            "far": split(far),
            "weights": entire(first["weights"]),
            "bias": entire(bias),
            "valid": entire(valid_mask),
            "bias_pick": bias_pick,
            "pick0": picked(1, 0),
            "pick1": picked(1, 1),
            "place": constant(np.concatenate(place)),
        },
        {
            "win_p": tokens_of(2 * WIN),
            "win_g": tokens_of(2 * WIN),
            "west": strip_of(CORNER),
            "north": strip_of(STRIP),
            "corner": strip_of(CORNER),
            "sum": wide_sum,
        },
        {"tables": pltpu.VMEM((2, WIN, LANES), F32)},
    )
    north = shift(below["north"], -1, 0)
    far_back = shift(below["corner"], -1, -1)
    west = shift(below["west"], 0, -1)
    last = attend(
        last_kernel,
        "attend_last",
        steps,
        common
        | {
            "fields": (fields, upper),
            "cot": (cotangent, upper),
            "weights": entire(first["weights"]),
            "table": entire(first["table"]),
            "west": entire(west0),
            "sum0": in_place(first["sum"]),
            "sum1": in_place(below["sum"]),
            "bias_pick": in_place(bias_pick[0]),
            "pick0": picked(0, 0),
        },
        {
            "win_p": half,
            "win_g": half,
            "west_p": tokens_of(WEST),
            "west_g": tokens_of(WEST),
            "bias_out": entire(shape_of(parts, WIN, 2 * ROWS)),
        },
        {
            "sum0_here": pltpu.VMEM((WIN, LANES), F32),
            "sum1_here": pltpu.VMEM((WIN, LANES), F32),
            "bias_pick_here": pltpu.VMEM((parts * ROWS, LANES), BF16),
            "arrived": pltpu.SemaphoreType.DMA((3,)),
        },
    )
    bias_sums = lax.all_to_all(last["bias_out"], "lon", 0, 0, tiled=True)

    out_bias = shape_of(HEADS * per, 2, WIN, kind=F32)
    steps, group = 2, pairs // 2
    block = paired(shape_of(*fields.shape), WZ * group)
    mixed, grad = call(
        land_kernel,
        "land",
        steps,
        [
            paired(fields, WZ * group),
            paired(cotangent, WZ * group),
            entire(first["in_p"]),
            entire(first["in_g"]),
            entire(last["win_p"]),
            entire(last["win_g"]),
            split(first["win_p"]),
            split(first["win_g"]),
            split(below["win_p"]),
            split(below["win_g"]),
            split(last["west_p"]),
            split(last["west_g"]),
            split(west),
            split(north),
            split(far_back),
            constant(land_picks()),
        ],
        [block, block],
        flops=10**11,
    )
    (grad_bias,) = call(bias_kernel, "bias_sum", 1, [entire(bias_sums)], [entire(out_bias)])
    grad_bias = grad_bias.reshape(HEADS, per, 2, WIN).transpose(2, 0, 1, 3)
    return mixed.transpose(0, 2, 1, 3), grad.transpose(0, 2, 1, 3), grad_bias


def solution(mesh):
    in_specs = (
        P(None, "lat", "lon", None),
        P(None, "lat", "lon", None),
        P(),
        P(),
        P(),
        P(None, None, "lon", None),
        P(),
        P(),
    )
    out_specs = (
        P(None, "lat", "lon", None),
        P(None, "lat", "lon", None),
        P("lat", None, "lon", None),
    )
    return jax.shard_map(local, mesh=mesh, in_specs=in_specs, out_specs=out_specs, check_vma=False)
```
